128 devices in a mesh: track: 4 (over x_lo, core), rows: 32 (over z, y, x_hi).
Axes of the slice: x: 4 (x_hi: 2, x_lo: 2; x = x_hi * 2 + x_lo), y: 4, z: 4, core: 2. Of those that a mesh axis runs over, the one named last changes fastest.
Arguments:
- homolog_embedding: bfloat16 [512, 512, 256], P('rows', 'track'), may hold values from -6 to 6
- couple_embedding: bfloat16 [512, 512, 128], P('rows', 'track'), may hold values from -6 to 6
- amino_validity_flags: int32 [512], replicated, may hold values 0 or 1
- homolog_validity_flags: int32 [512], replicated, may hold values 0 or 1
- strand_label: int32 [512], replicated, may hold values from 0 to 3, never falling along the last dimension, each value on 1 to 256 neighbouring positions
- focus_four_matrices: bfloat16 [256, 1024], replicated, may hold values from -0.375 to 0.375
- couple_offset_matrix: float32 [128, 8], replicated, may hold values from -30 to 30
- strand_couple_offset: float32 [8], replicated, may hold values from -5 to 5
- focus_final_matrix: bfloat16 [256, 256], replicated, may hold values from -2.390625 to 2.390625
- transit_expand_matrix: bfloat16 [256, 1024], replicated, may hold values from -0.375 to 0.375
- transit_shrink_matrix: bfloat16 [1024, 256], replicated, may hold values from -0.1875 to 0.1875
- tensor_average_factor_matrices: bfloat16 [256, 64], replicated, may hold values from -0.375 to 0.375
- tensor_average_final_matrix: bfloat16 [1024, 128], replicated, may hold values from -11 to 11
- trilateral_entry_matrices: bfloat16 [128, 512], replicated, may hold values from -0.5 to 0.5
- trilateral_sigmoid_matrix: bfloat16 [128, 128], replicated, may hold values from -0.5 to 0.5
- trilateral_final_matrix: bfloat16 [128, 128], replicated, may hold values from -0.5 to 0.5
Outputs:
- alignment_output: bfloat16 [512, 512, 256], P('rows', 'track')
- pair_output: bfloat16 [512, 512, 128], P('rows', 'track')
The draws below stay inside these ranges and needn't reach their ends.
Inputs may be any that keep to these rules, and one draw needn't show every extreme that they name: `strand_label`: chain numbers never fall along the residues; one chain holds exactly 256 residues.
All inputs are finite; a program needn't handle non-finite values.
Results may differ from the reference program's by a relative error of at most 0.02.
The reference program's roundings to bfloat16 on the way count: a program that leaves them out, or rounds other values in their place, can miss the bound.
Values may be sent and summed in bfloat16 or wider, within the bound.
No kernel may reach another device: no remote copies, remote signals or barrier semaphores. Data moves between devices by JAX's collectives and lax.ppermute only.
A program may use at most 192 MiB of HBM per device.

```python
import math
import jax
import jax.numpy as jnp
import numpy as np
from jax import lax

ALIGNED_FEATURES = 256
CZ = 128
CH = 128
FOCUS_SPLITS = 8
FOCUS_SPLIT_SIZE = 32
OPM_FACTOR_DIM = 32
TRANSIT_UNITS = 1024
RES_DEV = 16
HOMOLOG_NUMBER = 512
AMINO_NUMBER = 512


def draw_couple_offset_matrix(key, part):
    key = jax.random.fold_in(key, 11)
    base = jnp.clip(jax.random.normal(key, (CZ, FOCUS_SPLITS), jnp.float32), -4.0, 4.0) / math.sqrt(CZ)
    return base


def with_ends(values, stream_key, least, top_value):
    dims = values.shape
    place = [jax.random.randint(jax.random.fold_in(stream_key, axis), (), 0, dims[axis]) for axis in range(len(dims))]
    values = values.at[tuple(place)].set(least)
    longest = dims.index(max(dims))
    place[longest] = (place[longest] + 1) % dims[longest]
    return values.at[tuple(place)].set(top_value)


def steps_of(rng, shape, shards, least, largest):
    factor_of = 1.0
    for axis_at, blocks in shards:
        steps = jax.random.uniform(jax.random.fold_in(jax.random.fold_in(rng, 6), axis_at), (blocks,), jnp.float32, least / len(shards), largest / len(shards))
        factor_of = factor_of * jnp.repeat(jnp.exp(steps), shape[axis_at] // blocks).reshape((-1,) + (1,) * (len(shape) - 1 - axis_at))
    return factor_of


def length_profile(count, total, bound, slope):
    weights = [(1 << 20) // math.isqrt(rank ** slope) + 1 for rank in range(2, count + 1)]
    rest, counts = total - bound - (count - 1), [1] * (count - 1)
    while rest > 0:
        movable = [i for i in range(count - 1) if counts[i] < bound]
        mass, remaining = sum([weights[i] for i in movable]), rest
        for i in movable:
            more = min(bound - counts[i], max(1, remaining * weights[i] // mass), rest)
            counts[i] = counts[i] + more
            rest = rest - more
    return np.array([bound] + counts)


def uneven(own_key, number_of, total, bound, skew):
    if number_of == 2:
        one = jax.random.randint(own_key, (), max(1, total - bound), min(bound, total - 1) + 1)
        return jnp.stack([one, total - one])
    sizes = jnp.asarray(length_profile(number_of, total, bound, skew), jnp.int32)
    pairs = (number_of - 1) // 2
    donor, taker = sizes[1:1 + 2 * pairs:2], sizes[2:2 + 2 * pairs:2]
    room = jnp.minimum(donor - 1, bound - taker)
    passed = jax.random.randint(jax.random.fold_in(own_key, 1), (pairs,), 0, 1 << 20) % (room + 1)
    sizes = sizes.at[1:1 + 2 * pairs:2].set(donor - passed).at[2:2 + 2 * pairs:2].set(taker + passed)
    return sizes[jax.random.permutation(jax.random.fold_in(own_key, 2), number_of)]


def normal_values(own_key, extent, spread, bound, split=(), kind=jnp.bfloat16):
    factor_of = steps_of(own_key, extent, split, -0.22, 0.18) if split else 1.0
    drawn = jax.random.normal(own_key, extent, jnp.float32) * spread * factor_of
    return jnp.minimum(jnp.maximum(drawn, -bound), bound).astype(kind)


def setup_inputs(seed: int = 0) -> dict:
    splits = jax.random.split(jax.random.key(seed), 17)
    homolog_embedding = normal_values(splits[0], (HOMOLOG_NUMBER, AMINO_NUMBER, ALIGNED_FEATURES), 1.0, 6.0, ((0, 32), (1, 4)))
    couple_embedding = normal_values(splits[1], (AMINO_NUMBER, AMINO_NUMBER, CZ), 1.0, 6.0, ((0, 32), (1, 4)))
    amino_validity_flags = with_ends((jax.random.randint(splits[2], (AMINO_NUMBER,), 0, 8) < 7).astype(jnp.int32), jax.random.fold_in(splits[2], 1), 0, 1)
    homolog_validity_flags = with_ends((jax.random.randint(splits[3], (HOMOLOG_NUMBER,), 0, 4) < 3).astype(jnp.int32), jax.random.fold_in(splits[3], 1), 0, 1)
    strand_label = jnp.searchsorted(jnp.cumsum(uneven(splits[4], 4, AMINO_NUMBER, AMINO_NUMBER // 2, 1)), jnp.arange(AMINO_NUMBER), side="right").astype(jnp.int32)
    focus_four_matrices = normal_values(splits[5], (ALIGNED_FEATURES, 4 * FOCUS_SPLITS * FOCUS_SPLIT_SIZE), ALIGNED_FEATURES ** -0.5, 0.375)
    couple_offset_matrix = draw_couple_offset_matrix(jax.random.fold_in(splits[16], 71), 0)
    strand_couple_offset = jnp.clip(jax.random.uniform(splits[7], (FOCUS_SPLITS,), jnp.float32, -5.0, 5.0), -5.0, 5.0)
    focus_final_matrix = normal_values(splits[8], (FOCUS_SPLITS * FOCUS_SPLIT_SIZE, ALIGNED_FEATURES), 0.4, 2.390625)
    transit_expand_matrix = normal_values(splits[9], (ALIGNED_FEATURES, TRANSIT_UNITS), ALIGNED_FEATURES ** -0.5, 0.375)
    transit_shrink_matrix = normal_values(splits[10], (TRANSIT_UNITS, ALIGNED_FEATURES), TRANSIT_UNITS ** -0.5, 0.1875)
    tensor_average_factor_matrices = normal_values(splits[11], (ALIGNED_FEATURES, 2 * OPM_FACTOR_DIM), ALIGNED_FEATURES ** -0.5, 0.375)
    tensor_average_final_matrix = normal_values(splits[12], (OPM_FACTOR_DIM * OPM_FACTOR_DIM, CZ), (2.6 * HOMOLOG_NUMBER ** 0.5 / OPM_FACTOR_DIM), 11.0)
    trilateral_entry_matrices = normal_values(splits[13], (CZ, 4 * CH), CZ ** -0.5, 0.5)
    trilateral_sigmoid_matrix = normal_values(splits[14], (CZ, CZ), CZ ** -0.5, 0.5)
    trilateral_final_matrix = normal_values(splits[15], (CH, CZ), CH ** -0.5, 0.5)
    return {"homolog_embedding": homolog_embedding, "couple_embedding": couple_embedding, "amino_validity_flags": amino_validity_flags, "homolog_validity_flags": homolog_validity_flags, "strand_label": strand_label, "focus_four_matrices": focus_four_matrices, "couple_offset_matrix": couple_offset_matrix, "strand_couple_offset": strand_couple_offset, "focus_final_matrix": focus_final_matrix, "transit_expand_matrix": transit_expand_matrix, "transit_shrink_matrix": transit_shrink_matrix, "tensor_average_factor_matrices": tensor_average_factor_matrices, "tensor_average_final_matrix": tensor_average_final_matrix, "trilateral_entry_matrices": trilateral_entry_matrices, "trilateral_sigmoid_matrix": trilateral_sigmoid_matrix, "trilateral_final_matrix": trilateral_final_matrix}


norm_eps = 1e-05
mask_fill = 1000000000.0

def standardize_features(values):
    values = values.astype(jnp.float32)
    centered = values - lax.optimization_barrier(jnp.mean(values, axis=-1, keepdims=True))
    variance = lax.optimization_barrier(jnp.mean(centered * centered, axis=-1, keepdims=True))
    return centered * lax.rsqrt(variance + norm_eps)

def raveled_tensor_outcome(values, weight):
    lead = values.shape[:-1]
    result = jnp.dot(values.reshape(-1, values.shape[-1]), weight, preferred_element_type=jnp.float32)
    return result.reshape(lead + (weight.shape[1],))

def precise_outcome(values, weight):
    lead = values.shape[:-1]
    result = jnp.dot(values.reshape(-1, values.shape[-1]), weight, precision=lax.Precision.HIGHEST, preferred_element_type=jnp.float32)
    return result.reshape(lead + (weight.shape[1],))

def reference(homolog_embedding, couple_embedding, amino_validity_flags, homolog_validity_flags, strand_label, focus_four_matrices, couple_offset_matrix, strand_couple_offset, focus_final_matrix, transit_expand_matrix, transit_shrink_matrix, tensor_average_factor_matrices, tensor_average_final_matrix, trilateral_entry_matrices, trilateral_sigmoid_matrix, trilateral_final_matrix):
    res_live = amino_validity_flags.astype(jnp.float32)
    row_present = homolog_validity_flags.astype(jnp.float32)
    pair_norm = standardize_features(couple_embedding).astype(jnp.bfloat16)
    bias_terms = precise_outcome(pair_norm.astype(jnp.float32), couple_offset_matrix.astype(jnp.float32))
    same_chain = (strand_label[:, None] == strand_label[None, :]).astype(jnp.float32)
    pair_bias = (jnp.transpose(bias_terms, (2, 0, 1)) + strand_couple_offset[:, None, None] * same_chain[None]).astype(jnp.float32)
    homolog_standardized = standardize_features(homolog_embedding).astype(jnp.bfloat16)
    query_key_value_gate = raveled_tensor_outcome(homolog_standardized, focus_four_matrices).astype(jnp.bfloat16).reshape(HOMOLOG_NUMBER, AMINO_NUMBER, 4, FOCUS_SPLITS, FOCUS_SPLIT_SIZE)
    key_mask = (res_live - 1.0) * mask_fill
    score_scale = 1.0 / math.sqrt(FOCUS_SPLIT_SIZE)

    def attend_row(inputs):
        query, keys, values = inputs
        scores = jnp.einsum('ihd,jhd->hij', query.astype(jnp.float32), keys.astype(jnp.float32)) * score_scale
        scores = scores + pair_bias + key_mask[None, None, :]
        shifted = jnp.exp(scores - lax.optimization_barrier(jnp.max(scores, axis=-1, keepdims=True)))
        soft_weights = (shifted / lax.optimization_barrier(jnp.sum(shifted, axis=-1, keepdims=True))).astype(jnp.bfloat16)
        return jnp.einsum('hij,jhd->ihd', soft_weights.astype(jnp.float32), values.astype(jnp.float32))
    attended = lax.map(attend_row, (query_key_value_gate[:, :, 0], query_key_value_gate[:, :, 1], query_key_value_gate[:, :, 2]))
    sigmoid_scaled_result = (jax.nn.sigmoid(query_key_value_gate[:, :, 3].astype(jnp.float32)) * attended).astype(jnp.bfloat16).reshape(HOMOLOG_NUMBER, AMINO_NUMBER, FOCUS_SPLITS * FOCUS_SPLIT_SIZE)
    homolog_transit_between = homolog_embedding.astype(jnp.float32) + raveled_tensor_outcome(sigmoid_scaled_result, focus_final_matrix)
    hidden_state = jax.nn.relu(raveled_tensor_outcome(standardize_features(homolog_transit_between).astype(jnp.bfloat16), transit_expand_matrix)).astype(jnp.bfloat16)
    alignment_output = (homolog_transit_between + raveled_tensor_outcome(hidden_state, transit_shrink_matrix)).astype(jnp.bfloat16)
    side_projections = raveled_tensor_outcome(standardize_features(alignment_output).astype(jnp.bfloat16), tensor_average_factor_matrices)
    side_projections = (side_projections * (row_present[:, None] * res_live[None, :])[:, :, None]).astype(jnp.bfloat16)
    left_side = side_projections[:, :, :OPM_FACTOR_DIM]
    right_flat = side_projections[:, :, OPM_FACTOR_DIM:].reshape(HOMOLOG_NUMBER, AMINO_NUMBER * OPM_FACTOR_DIM).astype(jnp.float32)
    left_blocks = jnp.transpose(left_side.reshape(HOMOLOG_NUMBER, AMINO_NUMBER // RES_DEV, RES_DEV, OPM_FACTOR_DIM), (1, 0, 2, 3))

    def outer_block(block):
        flat_left = block.reshape(HOMOLOG_NUMBER, RES_DEV * OPM_FACTOR_DIM).astype(jnp.float32)
        outer_prod = jnp.einsum('sa,sb->ab', flat_left, right_flat).astype(jnp.bfloat16)
        arranged = jnp.transpose(outer_prod.reshape(RES_DEV, OPM_FACTOR_DIM, AMINO_NUMBER, OPM_FACTOR_DIM), (0, 2, 1, 3)).reshape(RES_DEV * AMINO_NUMBER, OPM_FACTOR_DIM * OPM_FACTOR_DIM)
        return jnp.dot(arranged, tensor_average_final_matrix, preferred_element_type=jnp.float32).reshape(RES_DEV, AMINO_NUMBER, CZ)
    opm_raw = lax.map(outer_block, left_blocks).reshape(AMINO_NUMBER, AMINO_NUMBER, CZ)
    pair_total_count = jnp.sum(row_present) * res_live[:, None] * res_live[None, :]
    opm_update = opm_raw / jnp.maximum(pair_total_count, 1.0)[:, :, None]
    pair_mid = (couple_embedding.astype(jnp.float32) + opm_update).astype(jnp.bfloat16)
    tri_norm = standardize_features(pair_mid).astype(jnp.bfloat16)
    projected = raveled_tensor_outcome(tri_norm, trilateral_entry_matrices).reshape(AMINO_NUMBER, AMINO_NUMBER, 4, CH)
    pair_live = (res_live[:, None] * res_live[None, :])[:, :, None]
    tri_left = (jax.nn.sigmoid(projected[:, :, 1]) * projected[:, :, 0] * pair_live).astype(jnp.bfloat16)
    tri_right = (jax.nn.sigmoid(projected[:, :, 3]) * projected[:, :, 2] * pair_live).astype(jnp.bfloat16)
    tri_sum = jnp.einsum('ikc,jkc->ijc', tri_left.astype(jnp.float32), tri_right.astype(jnp.float32))
    tri_sum_norm = standardize_features(tri_sum).astype(jnp.bfloat16)
    tri_update = raveled_tensor_outcome(tri_sum_norm, trilateral_final_matrix)
    tri_gate = jax.nn.sigmoid(raveled_tensor_outcome(tri_norm, trilateral_sigmoid_matrix))
    pair_output = (pair_mid.astype(jnp.float32) + tri_gate * tri_update).astype(jnp.bfloat16)
    return (alignment_output, pair_output)
```

```python
import functools
import math

import jax
import jax.numpy as jnp
from jax import lax
from jax.experimental import pallas as pl
from jax.experimental.pallas import tpu as pltpu
from jax.sharding import PartitionSpec as P

norm_eps = 1e-05
mask_fill = 1000000000.0
LOG2E = math.log2(math.e)
F32 = jnp.float32
BF16 = jnp.bfloat16
VLIM = 56 * 1024 * 1024
VMEM = pl.BlockSpec(memory_space=pltpu.VMEM)
SMEM = pl.BlockSpec(memory_space=pltpu.SMEM)


def lane_norm(x):
    x = x.astype(F32)
    x = x - jnp.mean(x, axis=-1, keepdims=True)
    var = jnp.mean(x * x, axis=-1, keepdims=True)
    return x * lax.rsqrt(var + norm_eps)


def row_norm(x):
    x = x - jnp.mean(x, axis=0, keepdims=True)
    var = jnp.mean(x * x, axis=0, keepdims=True)
    return x * lax.rsqrt(var + norm_eps)


def mm(a, b):
    return jnp.dot(a, b, preferred_element_type=F32)


def mm_nt(a, b):
    return lax.dot_general(a, b, (((1,), (1,)), ((), ())), preferred_element_type=F32)


def sigmoid(x):
    return 1.0 / (1.0 + jnp.exp(-x))


def call(body, outs, scratch=(), **kw):
    cost = kw.pop("cost", None)
    return pl.pallas_call(
        body,
        out_shape=outs,
        scratch_shapes=list(scratch),
        cost_estimate=cost,
        compiler_params=pltpu.CompilerParams(vmem_limit_bytes=VLIM),
        **kw,
    )


def bias_body(c_ref, w_ref, so_ref, same_ref, mask_ref, o_ref):
    rows = c_ref.shape[0]
    pn = lane_norm(c_ref[...]).astype(BF16).reshape(rows * 128, 128)
    b = mm_nt(w_ref[...], pn)
    b = b[0:8] + b[8:16] + b[16:24]
    so = so_ref[...]
    mask = mask_ref[...]
    for i in range(rows):
        o_ref[:, i, :] = b[:, i * 128 : (i + 1) * 128] + so * same_ref[i : i + 1, :] + mask


def attention_body(t_ref, x0, x1, x2, x3, w_ref, b_ref, o_ref, bias, scale):
    t = t_ref[0]

    @pl.when(pl.program_id(0) == 0)
    def _():
        for ki in range(4):
            for kj in range(4):

                @pl.loop(0, 8)
                def _(rr):
                    for h in range(2):
                        row = pl.multiple_of(ki * 128 + rr * 16, 16)
                        bias[h, pl.ds(row, 16), kj * 128 : (kj + 1) * 128] = b_ref[
                            (ki ^ t) * 8 + rr, kj ^ t, h
                        ]

    lane = lax.broadcasted_iota(jnp.int32, (1, 128), 1)
    factor = jnp.where(lane < 64, scale, 1.0)
    parts = [[], [], [], []]
    for s in range(2):
        xn = jnp.concatenate([lane_norm(x[s]).astype(BF16) for x in (x0, x1, x2, x3)], axis=0)
        qkvg = mm(xn, w_ref[...])
        qk = (qkvg[:, :128] * factor).astype(BF16)
        vg = qkvg[:, 128:].astype(BF16)
        q_moved = pltpu.roll(qk.astype(F32), 64, 1)
        gate = sigmoid(vg.astype(F32)[:, 64:])
        lhs, rhs = [], []
        for h in range(2):
            klanes = (lane >= 64 + 32 * h) & (lane < 96 + 32 * h)
            lhs.append(jnp.where(klanes, q_moved, 0.0).astype(BF16))
            vlanes = (lane >= 32 * h) & (lane < 32 + 32 * h)
            rhs.append(jnp.where(vlanes, vg.astype(F32), 1.0).astype(BF16))
        for k in range(4):
            lo, hi = k * 128, (k + 1) * 128
            outs = []
            for h in range(2):
                scores = mm_nt(lhs[h][lo:hi], qk) + bias[h, lo:hi, :]
                top = jnp.max(scores, axis=-1, keepdims=True)
                p = jnp.exp2(scores - top).astype(BF16)
                outs.append(mm(p, rhs[h]))
            head0 = lane < 32
            num = jnp.where(head0, outs[0], outs[1])[:, :64]
            den = jnp.where(head0[:, :64], outs[0][:, 64:], outs[1][:, 64:])
            parts[k].append(num / den * gate[lo:hi])
    for k in range(4):
        o_ref[k ^ t, 0] = jnp.concatenate(parts[k], axis=1).astype(BF16)


def transition_body(
    g_ref, x_ref, wo_ref, w1_ref, w2_ref, wl_ref, wr_ref, seq_ref, col_ref, row_ref,
    o_ref, l_ref, r_ref, lacc, racc,
):
    step = pl.program_id(0)
    gg = jnp.concatenate([g_ref[k, 0] for k in range(4)], axis=1)
    y = mm(gg, wo_ref[...])
    mid = jnp.concatenate(
        [x_ref[s].astype(F32) + y[:, s * 256 : (s + 1) * 256] for s in range(2)], axis=0
    )
    hidden = jnp.maximum(mm(lane_norm(mid).astype(BF16), w1_ref[...]), 0.0).astype(BF16)
    out = (mid + mm(hidden, w2_ref[...])).astype(BF16)
    z = lane_norm(out).astype(BF16)
    left = mm(z, wl_ref[...])
    rows = lax.broadcasted_iota(jnp.int32, (128, 128), 0)
    lanes = lax.broadcasted_iota(jnp.int32, (128, 128), 1)
    own = (rows % 4) == (lanes // 32)
    pick = (
        lax.broadcasted_iota(jnp.int32, (32, 128), 1) // 4
        == lax.broadcasted_iota(jnp.int32, (32, 128), 0)
    ).astype(BF16)
    place = lax.broadcasted_iota(jnp.int32, (1, 16, 1), 1)
    for s in range(2):
        o_ref[s] = out[s * 128 : (s + 1) * 128]
        live = seq_ref[2 * step + s]
        ls = (left[s * 128 : (s + 1) * 128] * (live * row_ref[...])).astype(BF16)
        ls = jnp.where(own, ls.astype(F32), 0.0).astype(BF16)
        flat = mm(pick, ls)
        rs = mm_nt(wr_ref[...], z[s * 128 : (s + 1) * 128]) * (live * col_ref[...])
        here = place == 2 * step + s
        lacc[...] = jnp.where(here, flat[:, None, :], lacc[...])
        racc[...] = jnp.where(here, rs[:, None, :], racc[...])

    @pl.when(step == pl.num_programs(0) - 1)
    def _():
        l_ref[...] = lacc[...].astype(BF16)
        r_ref[...] = racc[...].astype(BF16)


def outer_body(
    r_pos, a0, a1, a2, a3, b0, b1, b2, b3, l_ref, c_ref, w_ref, we_ref, inv_ref, live_ref,
    pm_ref, tn_ref, o_ref, la, lb, right, stack, lacc, racc,
):
    r = r_pos[0]
    for kz in range(4):
        for ky in range(4):
            for kx in range(2):
                src = r ^ (kz * 8 + ky * 2 + kx)
                at = (kz * 8 + ky * 2 + kx) * 16
                bt = (ky * 8 + kz * 2 + kx) * 16
                for g in range(4):
                    piece = l_ref[src, g]
                    la[at : at + 16, g * 128 : (g + 1) * 128] = piece
                    lb[bt : bt + 16, g * 128 : (g + 1) * 128] = piece
    for q, (a, b) in enumerate(zip((a0, a1, a2, a3), (b0, b1, b2, b3))):
        for n in range(16):
            right[q * 128 : (q + 1) * 128, n * 128 : (n + 1) * 128] = a[n].reshape(128, 128)
            m = n + 16
            right[q * 128 : (q + 1) * 128, m * 128 : (m + 1) * 128] = b[n].reshape(128, 128)
    for half, left in enumerate((la, lb)):
        lt = left[...].T
        for n in range(4):
            at = half * 16 + n * 4
            o = mm(lt, right[:, at * 128 : (at + 4) * 128]).astype(BF16)
            for q in range(4):
                for i in range(16):
                    stack[i, (at + q) * 32 : (at + q + 1) * 32, :] = o[
                        i * 32 : (i + 1) * 32, q * 128 : (q + 1) * 128
                    ]
    for i in range(16):
        update = mm(w_ref[...], stack[i])
        pm = (c_ref[i].astype(F32).T + update * inv_ref[i : i + 1, :]).astype(BF16)
        tn = row_norm(pm.astype(F32)).astype(BF16)
        pm_ref[i] = pm
        tn_ref[i] = tn
        proj = mm(we_ref[...], tn)
        live = live_ref[i : i + 1, :]
        lacc[:, i, :] = sigmoid(proj[128:256]) * proj[0:128] * live
        racc[:, i, :] = sigmoid(proj[384:512]) * proj[256:384] * live
    o_ref[:, 0] = lacc[...].astype(BF16)
    o_ref[:, 1] = racc[...].astype(BF16)


def triangle_body(x_ref, o_ref, left, right):
    for r in range(32):
        for t in range(4):
            left[r * 16 : (r + 1) * 16, t * 128 : (t + 1) * 128] = x_ref[r * 4 + t, 0]
            right[r * 16 : (r + 1) * 16, t * 128 : (t + 1) * 128] = x_ref[r * 4 + t, 1]
    for q in range(4):
        total = mm_nt(left[q * 128 : (q + 1) * 128, :], right[...])
        for r in range(8):
            for t in range(4):
                o_ref[(q * 8 + r) * 4 + t] = total[
                    r * 16 : (r + 1) * 16, t * 128 : (t + 1) * 128
                ].astype(o_ref.dtype)


def final_body(x_ref, pm_ref, tn_ref, wf_ref, wg_ref, o_ref, normed):
    normed[...] = row_norm(x_ref[...].astype(F32))
    for i in range(16):
        update = mm(wf_ref[...], normed[:, i, :].astype(BF16))
        gate = sigmoid(mm(wg_ref[...], tn_ref[i]))
        o_ref[i] = (pm_ref[i].astype(F32) + gate * update).T.astype(BF16)


def swap_rows(x, unit):
    return lax.ppermute(x, "rows", [(i, i ^ unit) for i in range(32)])


def swap_track(x, unit):
    return lax.ppermute(x, "track", [(i, i ^ unit) for i in range(4)])


def ring_gather(x, unit):
    one, three = swap_rows(x, unit), swap_rows(x, 3 * unit)
    half = x.shape[0] // 2
    first = swap_rows(three[:half], unit)
    second = swap_rows(one[half:], 3 * unit)
    return [x, one, jnp.concatenate([first, second], axis=0), three]


def local(
    homolog_embedding,
    couple_embedding,
    amino_validity_flags,
    homolog_validity_flags,
    strand_label,
    focus_four_matrices,
    couple_offset_matrix,
    strand_couple_offset,
    focus_final_matrix,
    transit_expand_matrix,
    transit_shrink_matrix,
    tensor_average_factor_matrices,
    tensor_average_final_matrix,
    trilateral_entry_matrices,
    trilateral_sigmoid_matrix,
    trilateral_final_matrix,
):
    t = lax.axis_index("track")
    r = lax.axis_index("rows")
    t_arr = t.astype(jnp.int32).reshape(1)
    r_arr = r.astype(jnp.int32).reshape(1)
    x2 = swap_track(homolog_embedding, 2)
    x1 = swap_track(homolog_embedding, 1)
    x3 = swap_track(x2, 1)

    res_live = amino_validity_flags.astype(F32)
    seq_live_all = homolog_validity_flags.astype(F32)
    col_live = lax.dynamic_slice_in_dim(res_live, t * 128, 128, 0)
    row_live = lax.dynamic_slice_in_dim(res_live, r * 16, 16, 0)
    seq_live = lax.dynamic_slice_in_dim(seq_live_all, r * 16, 16, 0)
    chain_cols = lax.dynamic_slice_in_dim(strand_label, t * 128, 128, 0)
    chain_rows = lax.dynamic_slice_in_dim(strand_label, r * 16, 16, 0)
    same_chain = (chain_rows[:, None] == chain_cols[None, :]).astype(F32)
    live_pair = row_live[:, None] * col_live[None, :]
    inv_count = 1.0 / jnp.maximum(jnp.sum(seq_live_all) * live_pair, 1.0)

    wb = (couple_offset_matrix * LOG2E).T
    hi = lax.reduce_precision(wb, 8, 7)
    mid = lax.reduce_precision(wb - hi, 8, 7)
    low = wb - hi - mid
    wb24 = jnp.concatenate([hi, mid, low], axis=0).astype(BF16)
    bias_local = call(bias_body, jax.ShapeDtypeStruct((8, 16, 128), F32))(
        couple_embedding,
        wb24,
        (strand_couple_offset * LOG2E).reshape(8, 1),
        same_chain,
        ((col_live - 1.0) * (mask_fill * LOG2E)).reshape(1, 128),
    )
    bias_send = jnp.broadcast_to(
        bias_local.reshape(1, 4, 2, 16, 128), (32, 4, 2, 16, 128)
    ).reshape(128, 2, 16, 128)
    bias_all = lax.all_to_all(bias_send, ("rows", "track"), 0, 0, tiled=True)

    w_heads = lax.dynamic_slice_in_dim(
        focus_four_matrices.reshape(256, 4, 8, 32), 2 * t, 2, 2
    ).reshape(256, 256)
    xspec = pl.BlockSpec((2, 128, 256), lambda n: (n, 0, 0))
    gated = call(
        functools.partial(attention_body, scale=LOG2E / math.sqrt(32.0)),
        jax.ShapeDtypeStruct((4, 8, 128, 128), BF16),
        [pltpu.VMEM((2, 512, 512), F32)],
        grid=(8,),
        in_specs=[
            SMEM, xspec, xspec, xspec, xspec,
            pl.BlockSpec((256, 256), lambda n: (0, 0)),
            pl.BlockSpec((32, 4, 2, 16, 128), lambda n: (0, 0, 0, 0, 0)),
        ],
        out_specs=pl.BlockSpec((4, 1, 128, 128), lambda n: (0, n, 0, 0)),
    )(
        t_arr, homolog_embedding, x1, x2, x3, w_heads, bias_all.reshape(32, 4, 2, 16, 128)
    )
    gated = lax.all_to_all(gated, "track", 0, 0, tiled=True)

    eye = jnp.eye(2, dtype=BF16)
    wo = (
        focus_final_matrix.reshape(4, 1, 64, 1, 256) * eye.reshape(1, 2, 1, 2, 1)
    ).reshape(512, 512)
    wl = jnp.tile(tensor_average_factor_matrices[:, :32], (1, 4))
    wr = tensor_average_factor_matrices[:, 32:].T
    whole = lambda *shape: pl.BlockSpec(shape, lambda n: (0,) * len(shape))
    alignment_output, left, right = call(
        transition_body,
        (
            jax.ShapeDtypeStruct((16, 128, 256), BF16),
            jax.ShapeDtypeStruct((32, 16, 128), BF16),
            jax.ShapeDtypeStruct((32, 16, 128), BF16),
        ),
        [pltpu.VMEM((32, 16, 128), F32), pltpu.VMEM((32, 16, 128), F32)],
        grid=(8,),
        in_specs=[
            pl.BlockSpec((4, 1, 128, 128), lambda n: (0, n, 0, 0)),
            xspec,
            whole(512, 512), whole(256, 1024), whole(1024, 256), whole(256, 128),
            whole(32, 256), SMEM, whole(1, 128), whole(128, 1),
        ],
        out_specs=(xspec, whole(32, 16, 128), whole(32, 16, 128)),
    )(
        gated, homolog_embedding, wo, transit_expand_matrix, transit_shrink_matrix, wl, wr,
        seq_live, col_live.reshape(1, 128), col_live.reshape(128, 1),
    )

    both = jnp.stack([right, swap_rows(right, 1)], axis=1)
    first = jnp.stack(ring_gather(both[:16], 2), axis=1)
    second = jnp.stack(ring_gather(both[16:], 8), axis=1)
    first = ring_gather(first, 8)
    second = ring_gather(second, 2)
    left_wide = lax.all_gather(left, "track", axis=0, tiled=True)
    left_all = lax.all_to_all(left_wide.reshape(32, 4, 16, 128), "rows", 0, 0, tiled=True)

    w_out = (
        tensor_average_final_matrix.reshape(32, 32, 128).transpose(2, 1, 0).reshape(128, 1024)
    )
    pair_mid, tri_norm, tri_sides = call(
        outer_body,
        (
            jax.ShapeDtypeStruct((16, 128, 128), BF16),
            jax.ShapeDtypeStruct((16, 128, 128), BF16),
            jax.ShapeDtypeStruct((128, 2, 16, 128), BF16),
        ),
        [
            pltpu.VMEM((512, 512), BF16),
            pltpu.VMEM((512, 512), BF16),
            pltpu.VMEM((512, 4096), BF16),
            pltpu.VMEM((16, 1024, 128), BF16),
            pltpu.VMEM((128, 16, 128), F32),
            pltpu.VMEM((128, 16, 128), F32),
        ],
        in_specs=[SMEM] + [VMEM] * 14,
        out_specs=(VMEM,) * 3,
    )(
        r_arr, *first, *second, left_all, couple_embedding, w_out,
        trilateral_entry_matrices.T, inv_count, live_pair,
    )

    tri_all = lax.all_to_all(tri_sides, ("rows", "track"), 0, 0, tiled=True)
    tri_sum = call(
        triangle_body,
        jax.ShapeDtypeStruct((128, 16, 128), F32),
        [pltpu.VMEM((512, 512), BF16), pltpu.VMEM((512, 512), BF16)],
        in_specs=[VMEM],
        out_specs=VMEM,
    )(tri_all)
    tri_back = lax.all_to_all(tri_sum, ("rows", "track"), 0, 0, tiled=True)
    pair_output = call(
        final_body,
        jax.ShapeDtypeStruct((16, 128, 128), BF16),
        [pltpu.VMEM((128, 16, 128), F32)],
        in_specs=[VMEM] * 5,
        out_specs=VMEM,
    )(tri_back, pair_mid, tri_norm, trilateral_final_matrix.T, trilateral_sigmoid_matrix.T)
    return (alignment_output, pair_output)


def solution(mesh):
    return jax.shard_map(
        local,
        mesh=mesh,
        in_specs=(P("rows", "track", None), P("rows", "track", None)) + (P(),) * 14,
        out_specs=(P("rows", "track", None), P("rows", "track", None)),
        check_vma=False,
    )
```

```python
import functools
import math

import jax
import jax.numpy as jnp
from jax import lax
from jax.experimental import pallas as pl
from jax.experimental.pallas import tpu as pltpu
from jax.sharding import PartitionSpec as P

norm_eps = 1e-05
mask_fill = 1000000000.0
LOG2E = math.log2(math.e)
F32 = jnp.float32
BF16 = jnp.bfloat16
VLIM = 56 * 1024 * 1024
VMEM = pl.BlockSpec(memory_space=pltpu.VMEM)
SMEM = pl.BlockSpec(memory_space=pltpu.SMEM)


def lane_norm(x):
    x = x.astype(F32)
    x = x - jnp.mean(x, axis=-1, keepdims=True)
    var = jnp.mean(x * x, axis=-1, keepdims=True)
    return x * lax.rsqrt(var + norm_eps)


def row_norm(x):
    x = x - jnp.mean(x, axis=0, keepdims=True)
    var = jnp.mean(x * x, axis=0, keepdims=True)
    return x * lax.rsqrt(var + norm_eps)


def mm(a, b):
    return jnp.dot(a, b, preferred_element_type=F32)


def mm_nt(a, b):
    return lax.dot_general(a, b, (((1,), (1,)), ((), ())), preferred_element_type=F32)


def sigmoid(x):
    return 1.0 / (1.0 + jnp.exp(-x))


def call(body, outs, scratch=(), **kw):
    cost = kw.pop("cost", None)
    return pl.pallas_call(
        body,
        out_shape=outs,
        scratch_shapes=list(scratch),
        cost_estimate=cost,
        compiler_params=pltpu.CompilerParams(vmem_limit_bytes=VLIM),
        **kw,
    )


def bias_body(pos_ref, chain_ref, c_ref, w_ref, so_ref, cols_ref, res_ref, o_ref, out, sem):
    t, r = pos_ref[0], pos_ref[1]
    rows = c_ref.shape[0]
    w = w_ref[...].T * LOG2E
    hi = w.astype(BF16)
    rest = w - hi.astype(F32)
    mid = rest.astype(BF16)
    low = (rest - mid.astype(F32)).astype(BF16)
    pn = lane_norm(c_ref[...]).astype(BF16).reshape(rows * 128, 128)
    b = mm_nt(hi, pn) + mm_nt(mid, pn) + mm_nt(low, pn)
    so = so_ref[...] * LOG2E
    chain = cols_ref[pl.ds(t, 1), :]
    mask = (res_ref[pl.ds(t, 1), :].astype(F32) - 1.0) * (mask_fill * LOG2E)
    for i in range(rows):
        same = (chain == chain_ref[r * rows + i]).astype(F32)
        out[:, i, :] = b[:, i * 128 : (i + 1) * 128] + so * same + mask
    copies = [pltpu.make_async_copy(out, o_ref.at[n], sem.at[n]) for n in range(32)]
    for c in copies:
        c.start()
    for c in copies:
        c.wait()


def project_body(x0, x1, x2, x3, w_ref, q_ref, k_ref, v_ref, g_ref, *, scale):
    lane = lax.broadcasted_iota(jnp.int32, (1, 128), 1)
    factor = jnp.where(lane < 64, scale, 1.0)
    gates = []
    for s in range(2):
        xn = jnp.concatenate([lane_norm(x[s]).astype(BF16) for x in (x0, x1, x2, x3)], axis=0)
        qkvg = mm(xn, w_ref[...])
        qk = qkvg[:, :128] * factor
        vg = qkvg[:, 128:].astype(BF16).astype(F32)
        k_ref[s] = qk.astype(BF16)
        moved = pltpu.roll(qk, 64, 1)
        for h in range(2):
            klanes = (lane >= 64 + 32 * h) & (lane < 96 + 32 * h)
            q_ref[h, s] = jnp.where(klanes, moved, 0.0).astype(BF16)
            vlanes = (lane >= 32 * h) & (lane < 32 + 32 * h)
            v_ref[h, s] = jnp.where(vlanes, vg, 1.0).astype(BF16)
        gates.append(vg)
    g_ref[0] = jnp.where(lane < 64, pltpu.roll(gates[0], 64, 1), gates[1]).astype(BF16)


def attention_body(t_ref, q_ref, k_ref, v_ref, g_ref, b_ref, o_ref, bias):
    t = t_ref[0]

    @pl.when(pl.program_id(0) == 0)
    def _():
        for ki in range(4):
            for kj in range(4):

                @pl.loop(0, 8)
                def _(rr):
                    for h in range(2):
                        row = pl.multiple_of(ki * 128 + rr * 16, 16)
                        bias[h, pl.ds(row, 16), kj * 128 : (kj + 1) * 128] = b_ref[
                            (ki ^ t) * 8 + rr, kj ^ t, h
                        ]

    size = 256
    blocks = [(s, k, h) for s in range(2) for k in range(512 // size) for h in range(2)]

    def score(block):
        s, k, h = block
        at = slice(k * size, (k + 1) * size)
        return mm_nt(q_ref[h, s, at], k_ref[s]) + bias[h, at, :]

    outs = {}

    def weigh(block, p):
        s, k, h = block
        outs[block] = mm(p, v_ref[h, s])

    following, held = score(blocks[0]), None
    for n, block in enumerate(blocks):
        now = following
        if n + 1 < len(blocks):
            following = score(blocks[n + 1])
        p = jnp.exp2(now - jnp.max(now, axis=-1, keepdims=True)).astype(BF16)
        if held is not None:
            weigh(*held)
        held = (block, p)
    weigh(*held)
    head0 = lax.broadcasted_iota(jnp.int32, (1, 128), 1) < 32
    for k in range(512 // size):
        at = slice(k * size, (k + 1) * size)
        parts = []
        for s in range(2):
            o0, o1 = outs[(s, k, 0)], outs[(s, k, 1)]
            num = jnp.where(head0, o0, o1)[:, :64]
            den = jnp.where(head0[:, :64], o0[:, 64:], o1[:, 64:])
            parts.append(num / den)
        y = jnp.concatenate(parts, axis=1) * sigmoid(g_ref[0, at].astype(F32))
        y = y.astype(BF16)
        for n in range(size // 128):
            o_ref[(k * (size // 128) + n) ^ t, 0] = y[n * 128 : (n + 1) * 128]


def transition_body(
    g_ref, x_ref, wo_ref, w1_ref, w2_ref, wl_ref, wr_ref, seq_ref, col_ref, row_ref,
    o_ref, l_ref, r_ref, lacc, racc,
):
    step = pl.program_id(0)
    gg = jnp.concatenate(
        [jnp.concatenate([g_ref[k, p] for k in range(4)], axis=1) for p in range(2)], axis=0
    )
    y = mm(gg, wo_ref[...])
    mid = jnp.concatenate(
        [
            x_ref[s].astype(F32)
            + y[(s // 2) * 128 : (s // 2 + 1) * 128, (s % 2) * 256 : (s % 2 + 1) * 256]
            for s in range(4)
        ],
        axis=0,
    )
    hidden = jnp.maximum(mm(lane_norm(mid).astype(BF16), w1_ref[...]), 0.0).astype(BF16)
    out = (mid + mm(hidden, w2_ref[...])).astype(BF16)
    z = lane_norm(out).astype(BF16)
    left = mm(z, wl_ref[...])
    right = mm_nt(wr_ref[...], z)
    rows = lax.broadcasted_iota(jnp.int32, (128, 128), 0)
    lanes = lax.broadcasted_iota(jnp.int32, (128, 128), 1)
    own = (rows % 4) == (lanes // 32)
    pick = (
        lax.broadcasted_iota(jnp.int32, (32, 128), 1) // 4
        == lax.broadcasted_iota(jnp.int32, (32, 128), 0)
    ).astype(BF16)
    for s in range(4):
        at = slice(s * 128, (s + 1) * 128)
        o_ref[s] = out[at]
        live = seq_ref[4 * step + s].astype(F32)
        ls = (left[at] * (live * row_ref[...].astype(F32))).astype(BF16)
        ls = jnp.where(own, ls.astype(F32), 0.0).astype(BF16)
        lacc[:, pl.ds(4 * step + s, 1), :] = mm(pick, ls)[:, None, :]
        rs = right[:, at] * (live * col_ref[...].astype(F32))
        racc[:, pl.ds(4 * step + s, 1), :] = rs[:, None, :]

    @pl.when(step == pl.num_programs(0) - 1)
    def _():
        l_ref[...] = lacc[...].astype(BF16)
        r_ref[...] = racc[...].astype(BF16)


def outer_body(
    r_pos, a0, a1, a2, a2b, a3, b0, b1, b2, b2b, b3, l_ref, c_ref, w_ref, we_ref, inv_ref, live_ref,
    pm_ref, tn_ref, o_ref, left, right, stack, lacc, racc, sem,
):
    r = r_pos[0]
    copies = []

    def fetch(src, dst):
        copies.append(pltpu.make_async_copy(src, dst, sem.at[len(copies)]))
        copies[-1].start()

    for k, parts in enumerate(((a0,), (a1,), (a2, a2b), (a3,))):
        n = 16 // len(parts)
        for m, part in enumerate(parts):
            fetch(part, right.at[pl.ds(m * n, n), k])
    for k, parts in enumerate(((b0,), (b1,), (b2, b2b), (b3,))):
        n = 16 // len(parts)
        for m, part in enumerate(parts):
            fetch(part, right.at[pl.ds(16 + m * n, n), :, k])
    for k in range(32):
        for g in range(4):
            left[k * 16 : (k + 1) * 16, g * 128 : (g + 1) * 128] = l_ref[r ^ k, g]
    lt = left[...].T
    for c in copies:
        c.wait()
    for n in range(8):
        cols = jnp.concatenate([right[n * 4 + q].reshape(512, 128) for q in range(4)], axis=1)
        o = mm(lt, cols).astype(BF16)
        for q in range(4):
            for i in range(16):
                stack[(n * 4 + q) * 32 : (n * 4 + q + 1) * 32, i * 128 : (i + 1) * 128] = o[
                    i * 32 : (i + 1) * 32, q * 128 : (q + 1) * 128
                ]
    for n in range(4):
        at = slice(n * 512, (n + 1) * 512)
        update = mm(w_ref[...], stack[:, at])
        ct = jnp.concatenate([c_ref[n * 4 + q].astype(F32).T for q in range(4)], axis=1)
        inv = jnp.concatenate([inv_ref[n * 4 + q : n * 4 + q + 1, :] for q in range(4)], axis=1)
        live = jnp.concatenate([live_ref[n * 4 + q : n * 4 + q + 1, :] for q in range(4)], axis=1)
        pm = (ct + update * inv).astype(BF16)
        tn = row_norm(pm.astype(F32)).astype(BF16)
        pm_ref[:, at] = pm
        tn_ref[:, at] = tn
        proj = mm(we_ref[...], tn)
        ls = sigmoid(proj[128:256]) * proj[0:128] * live
        rs = sigmoid(proj[384:512]) * proj[256:384] * live
        for q in range(4):
            lacc[:, n * 4 + q, :] = ls[:, q * 128 : (q + 1) * 128]
            racc[:, n * 4 + q, :] = rs[:, q * 128 : (q + 1) * 128]
    o_ref[:, 0] = lacc[...].astype(BF16)
    o_ref[:, 1] = racc[...].astype(BF16)


def triangle_body(x_ref, o_ref, left, right):
    for r in range(32):
        for t in range(4):
            left[r * 16 : (r + 1) * 16, t * 128 : (t + 1) * 128] = x_ref[r * 4 + t, 0]
            right[r * 16 : (r + 1) * 16, t * 128 : (t + 1) * 128] = x_ref[r * 4 + t, 1]
    for q in range(4):
        total = mm_nt(left[q * 128 : (q + 1) * 128, :], right[...])
        for r in range(8):
            for t in range(4):
                o_ref[(q * 8 + r) * 4 + t] = total[
                    r * 16 : (r + 1) * 16, t * 128 : (t + 1) * 128
                ].astype(o_ref.dtype)


def final_body(x_ref, pm_ref, tn_ref, wf_ref, wg_ref, o_ref, normed):
    normed[...] = row_norm(x_ref[...].astype(F32))
    for n in range(4):
        at = slice(n * 512, (n + 1) * 512)
        nt = jnp.concatenate([normed[:, n * 4 + q, :] for q in range(4)], axis=1)
        update = mm(wf_ref[...], nt.astype(BF16))
        gate = sigmoid(mm(wg_ref[...], tn_ref[:, at]))
        res = pm_ref[:, at].astype(F32) + gate * update
        for q in range(4):
            o_ref[n * 4 + q] = res[:, q * 128 : (q + 1) * 128].T.astype(BF16)


def swap_rows(x, unit):
    return lax.ppermute(x, "rows", [(i, i ^ unit) for i in range(32)])


def swap_track(x, unit):
    return lax.ppermute(x, "track", [(i, i ^ unit) for i in range(4)])


def ring_gather(x, unit):
    one, three = swap_rows(x, unit), swap_rows(x, 3 * unit)
    half = x.shape[0] // 2
    first = swap_rows(three[:half], unit)
    second = swap_rows(one[half:], 3 * unit)
    return [x, one, first, second, three]


def ring_stack(x, unit):
    own, one, first, second, three = ring_gather(x, unit)
    return jnp.stack([own, one, jnp.concatenate([first, second], axis=0), three], axis=1)


def local(
    homolog_embedding,
    couple_embedding,
    amino_validity_flags,
    homolog_validity_flags,
    strand_label,
    focus_four_matrices,
    couple_offset_matrix,
    strand_couple_offset,
    focus_final_matrix,
    transit_expand_matrix,
    transit_shrink_matrix,
    tensor_average_factor_matrices,
    tensor_average_final_matrix,
    trilateral_entry_matrices,
    trilateral_sigmoid_matrix,
    trilateral_final_matrix,
):
    t = lax.axis_index("track")
    r = lax.axis_index("rows")
    t_arr = t.astype(jnp.int32).reshape(1)
    r_arr = r.astype(jnp.int32).reshape(1)
    x2 = swap_track(homolog_embedding, 2)
    x1 = swap_track(homolog_embedding, 1)
    x3 = swap_track(x2, 1)

    bias_send = call(
        bias_body,
        jax.ShapeDtypeStruct((32, 8, 16, 128), F32),
        [pltpu.VMEM((8, 16, 128), F32), pltpu.SemaphoreType.DMA((32,))],
        in_specs=[SMEM, SMEM] + [VMEM] * 5,
        out_specs=pl.BlockSpec(memory_space=pl.ANY),
    )(
        jnp.stack([t, r]).astype(jnp.int32),
        strand_label,
        couple_embedding,
        couple_offset_matrix,
        strand_couple_offset.reshape(8, 1),
        strand_label.reshape(4, 128),
        amino_validity_flags.reshape(4, 128),
    )
    bias_all = lax.all_to_all(
        bias_send.reshape(128, 2, 16, 128), ("rows", "track"), 0, 0, tiled=True
    )

    w_heads = lax.dynamic_slice_in_dim(
        focus_four_matrices.reshape(256, 4, 8, 32), 2 * t, 2, 2
    ).reshape(256, 256)
    xspec = pl.BlockSpec((2, 128, 256), lambda n: (n, 0, 0))
    xspec4 = pl.BlockSpec((4, 128, 256), lambda n: (n, 0, 0))
    pair_spec = pl.BlockSpec((2, 2, 512, 128), lambda n: (0, n, 0, 0))
    one_spec = pl.BlockSpec((2, 512, 128), lambda n: (n, 0, 0))
    gate_spec = pl.BlockSpec((1, 512, 128), lambda n: (n, 0, 0))
    whole = lambda *shape: pl.BlockSpec(shape, lambda n: (0,) * len(shape))
    query, key, value, gate = call(
        functools.partial(project_body, scale=LOG2E / math.sqrt(32.0)),
        (
            jax.ShapeDtypeStruct((2, 16, 512, 128), BF16),
            jax.ShapeDtypeStruct((16, 512, 128), BF16),
            jax.ShapeDtypeStruct((2, 16, 512, 128), BF16),
            jax.ShapeDtypeStruct((8, 512, 128), BF16),
        ),
        grid=(8,),
        in_specs=[xspec, xspec, xspec, xspec, whole(256, 256)],
        out_specs=(pair_spec, one_spec, pair_spec, gate_spec),
        cost=pl.CostEstimate(
            flops=16 * 512 * 256 * 256 * 2, bytes_accessed=16 << 20, transcendentals=0
        ),
    )(homolog_embedding, x1, x2, x3, w_heads)
    gated = call(
        attention_body,
        jax.ShapeDtypeStruct((4, 8, 128, 128), BF16),
        [pltpu.VMEM((2, 512, 512), F32)],
        grid=(8,),
        in_specs=[
            SMEM, pair_spec, one_spec, pair_spec, gate_spec, whole(32, 4, 2, 16, 128),
        ],
        out_specs=pl.BlockSpec((4, 1, 128, 128), lambda n: (0, n, 0, 0)),
    )(t_arr, query, key, value, gate, bias_all.reshape(32, 4, 2, 16, 128))
    gated = lax.all_to_all(gated, "track", 0, 0, tiled=True)

    res_live = amino_validity_flags.astype(F32)
    seq_live_all = homolog_validity_flags.astype(F32)
    col_live = lax.dynamic_slice_in_dim(res_live, t * 128, 128, 0)
    row_live = lax.dynamic_slice_in_dim(res_live, r * 16, 16, 0)
    seq_live = lax.dynamic_slice_in_dim(seq_live_all, r * 16, 16, 0)
    live_pair = row_live[:, None] * col_live[None, :]
    inv_count = 1.0 / jnp.maximum(jnp.sum(seq_live_all) * live_pair, 1.0)
    eye = jnp.eye(2, dtype=BF16)
    wo = (
        focus_final_matrix.reshape(4, 1, 64, 1, 256) * eye.reshape(1, 2, 1, 2, 1)
    ).reshape(512, 512)
    wl = jnp.tile(tensor_average_factor_matrices[:, :32], (1, 4))
    wr = tensor_average_factor_matrices[:, 32:].T
    alignment_output, left, right = call(
        transition_body,
        (
            jax.ShapeDtypeStruct((16, 128, 256), BF16),
            jax.ShapeDtypeStruct((32, 16, 128), BF16),
            jax.ShapeDtypeStruct((32, 16, 128), BF16),
        ),
        [pltpu.VMEM((32, 16, 128), F32), pltpu.VMEM((32, 16, 128), F32)],
        grid=(4,),
        in_specs=[
            pl.BlockSpec((4, 2, 128, 128), lambda n: (0, n, 0, 0)),
            xspec4,
            whole(512, 512), whole(256, 1024), whole(1024, 256), whole(256, 128),
            whole(32, 256), SMEM, whole(1, 128), whole(128, 1),
        ],
        out_specs=(xspec4, whole(32, 16, 128), whole(32, 16, 128)),
    )(
        gated, homolog_embedding, wo, transit_expand_matrix, transit_shrink_matrix, wl, wr,
        seq_live, col_live.reshape(1, 128), col_live.reshape(128, 1),
    )

    both = jnp.stack([right, swap_rows(right, 1)], axis=1)
    first = ring_gather(ring_stack(both[:16], 2), 8)
    second = ring_gather(ring_stack(both[16:], 8), 2)
    first = [a.reshape(a.shape[0], 4, 32, 128) for a in first]
    second = [a.reshape(a.shape[0], 4, 32, 128) for a in second]
    left_wide = lax.all_gather(left, "track", axis=0, tiled=True)
    left_all = lax.all_to_all(left_wide.reshape(32, 4, 16, 128), "rows", 0, 0, tiled=True)

    w_out = (
        tensor_average_final_matrix.reshape(32, 32, 128).transpose(2, 1, 0).reshape(128, 1024)
    )
    pair_mid, tri_norm, tri_sides = call(
        outer_body,
        (
            jax.ShapeDtypeStruct((128, 2048), BF16),
            jax.ShapeDtypeStruct((128, 2048), BF16),
            jax.ShapeDtypeStruct((128, 2, 16, 128), BF16),
        ),
        [
            pltpu.VMEM((512, 512), BF16),
            pltpu.VMEM((32, 4, 4, 32, 128), BF16),
            pltpu.VMEM((1024, 2048), BF16),
            pltpu.VMEM((128, 16, 128), F32),
            pltpu.VMEM((128, 16, 128), F32),
            pltpu.SemaphoreType.DMA((10,)),
        ],
        in_specs=[SMEM] + [pl.BlockSpec(memory_space=pl.ANY)] * 10 + [VMEM] * 6,
        out_specs=(VMEM,) * 3,
    )(
        r_arr, *first, *second, left_all, couple_embedding, w_out,
        trilateral_entry_matrices.T, inv_count, live_pair,
    )

    tri_all = lax.all_to_all(tri_sides, ("rows", "track"), 0, 0, tiled=True)
    tri_sum = call(
        triangle_body,
        jax.ShapeDtypeStruct((128, 16, 128), BF16),
        [pltpu.VMEM((512, 512), BF16), pltpu.VMEM((512, 512), BF16)],
        in_specs=[VMEM],
        out_specs=VMEM,
    )(tri_all)
    tri_back = lax.all_to_all(tri_sum, ("rows", "track"), 0, 0, tiled=True)
    pair_output = call(
        final_body,
        jax.ShapeDtypeStruct((16, 128, 128), BF16),
        [pltpu.VMEM((128, 16, 128), F32)],
        in_specs=[VMEM] * 5,
        out_specs=VMEM,
    )(tri_back, pair_mid, tri_norm, trilateral_final_matrix.T, trilateral_sigmoid_matrix.T)
    return (alignment_output, pair_output)


def solution(mesh):
    return jax.shard_map(
        local,
        mesh=mesh,
        in_specs=(P("rows", "track", None), P("rows", "track", None)) + (P(),) * 14,
        out_specs=(P("rows", "track", None), P("rows", "track", None)),
        check_vma=False,
    )
```

```python
import functools
import math

import jax
import jax.numpy as jnp
from jax import lax
from jax.experimental import pallas as pl
from jax.experimental.pallas import tpu as pltpu
from jax.sharding import PartitionSpec as P

norm_eps = 1e-05
mask_fill = 1000000000.0
LOG2E = math.log2(math.e)
F32 = jnp.float32
BF16 = jnp.bfloat16
VMEM = pl.BlockSpec(memory_space=pltpu.VMEM)
SMEM = pl.BlockSpec(memory_space=pltpu.SMEM)


def lane_norm(x):
    x = x.astype(F32)
    x = x - jnp.mean(x, axis=-1, keepdims=True)
    var = jnp.mean(x * x, axis=-1, keepdims=True)
    return x * lax.rsqrt(var + norm_eps)


def row_norm(x):
    x = x - jnp.mean(x, axis=0, keepdims=True)
    var = jnp.mean(x * x, axis=0, keepdims=True)
    return x * lax.rsqrt(var + norm_eps)


def mm(a, b):
    return jnp.dot(a, b, preferred_element_type=F32)


def mm_nt(a, b):
    return lax.dot_general(a, b, (((1,), (1,)), ((), ())), preferred_element_type=F32)


def sigmoid(x):
    return 1.0 / (1.0 + jnp.exp(-x))


def call(body, outs, scratch=(), **kw):
    cost = kw.pop("cost", None)
    mib = kw.pop("mib")
    return pl.pallas_call(
        body,
        out_shape=outs,
        scratch_shapes=list(scratch),
        cost_estimate=cost,
        compiler_params=pltpu.CompilerParams(vmem_limit_bytes=mib * 1024 * 1024),
        **kw,
    )


def bias_body(chain_ref, so_ref, c_ref, w_ref, cols_ref, res_ref, o_ref, out, sem):
    t, r = lax.axis_index("track"), lax.axis_index("rows")
    rows = c_ref.shape[0]
    w = w_ref[...] * LOG2E
    hi = w.astype(BF16).astype(F32)
    mid = (w - hi).astype(BF16).astype(F32)
    w = jnp.concatenate([hi, mid, w - hi - mid], axis=0).astype(BF16)
    pn = lane_norm(c_ref[...]).astype(BF16).reshape(rows * 128, 128)
    b = mm_nt(w, pn)
    b = b[0:8] + b[8:16] + b[16:24]
    head = lax.broadcasted_iota(jnp.int32, (8, 1), 0)
    so = jnp.zeros((8, 1), F32)
    for h in range(8):
        so = jnp.where(head == h, so_ref[h], so)
    so = so * LOG2E
    chain = cols_ref[pl.ds(t, 1), :]
    mask = (res_ref[pl.ds(t, 1), :].astype(F32) - 1.0) * (mask_fill * LOG2E)
    for i in range(rows):
        same = (chain == chain_ref[r * rows + i]).astype(F32)
        out[:, i, :] = b[:, i * 128 : (i + 1) * 128] + so * same + mask
    copies = [pltpu.make_async_copy(out, o_ref.at[n], sem.at[n]) for n in range(32)]
    for c in copies:
        c.start()
    for c in copies:
        c.wait()


def project_body(x0, x1, x2, x3, w_ref, q_ref, k_ref, v_ref, g_ref, *, scale):
    lane = lax.broadcasted_iota(jnp.int32, (1, 128), 1)
    factor = jnp.where(lane < 64, scale, 1.0)
    gates = []
    for s in range(2):
        xn = jnp.concatenate([lane_norm(x[s]).astype(BF16) for x in (x0, x1, x2, x3)], axis=0)
        qkvg = mm(xn, w_ref[...])
        qk = qkvg[:, :128] * factor
        vg = qkvg[:, 128:].astype(BF16).astype(F32)
        k_ref[s] = qk.astype(BF16)
        moved = pltpu.roll(qk, 64, 1)
        for h in range(2):
            klanes = (lane >= 64 + 32 * h) & (lane < 96 + 32 * h)
            q_ref[h, s] = jnp.where(klanes, moved, 0.0).astype(BF16)
            vlanes = (lane >= 32 * h) & (lane < 32 + 32 * h)
            v_ref[h, s] = jnp.where(vlanes, vg, 1.0).astype(BF16)
        gates.append(vg)
    g_ref[0] = jnp.where(lane < 64, pltpu.roll(gates[0], 64, 1), gates[1]).astype(BF16)


def attention_body(q_ref, k_ref, v_ref, g_ref, b_ref, o_ref):
    t = lax.axis_index("track")
    size = 256
    blocks = [(s, k, h) for s in range(2) for k in range(512 // size) for h in range(2)]

    def bias(k, h):
        tall = []
        for ki in range(k * size // 128, (k + 1) * size // 128):
            rows = pl.ds(pl.multiple_of((ki ^ t) * 8, 8), 8)
            wide = [b_ref[rows, kj ^ t, h].reshape(128, 128) for kj in range(4)]
            tall.append(jnp.concatenate(wide, axis=1))
        return jnp.concatenate(tall, axis=0)

    def score(block):
        s, k, h = block
        return mm_nt(q_ref[h, s, k * size : (k + 1) * size], k_ref[s]) + bias(k, h)

    outs = {}

    def weigh(block, p):
        s, k, h = block
        outs[block] = mm(p, v_ref[h, s])

    following, held = score(blocks[0]), None
    for n, block in enumerate(blocks):
        now = following
        if n + 1 < len(blocks):
            following = score(blocks[n + 1])
        p = jnp.exp2(now - jnp.max(now, axis=-1, keepdims=True)).astype(BF16)
        if held is not None:
            weigh(*held)
        held = (block, p)
    weigh(*held)
    head0 = lax.broadcasted_iota(jnp.int32, (1, 128), 1) < 32
    for k in range(512 // size):
        at = slice(k * size, (k + 1) * size)
        parts = []
        for s in range(2):
            o0, o1 = outs[(s, k, 0)], outs[(s, k, 1)]
            num = jnp.where(head0, o0, o1)[:, :64]
            den = jnp.where(head0[:, :64], o0[:, 64:], o1[:, 64:])
            parts.append(num / den)
        y = jnp.concatenate(parts, axis=1) * sigmoid(g_ref[0, at].astype(F32))
        y = y.astype(BF16)
        for n in range(size // 128):
            o_ref[(k * (size // 128) + n) ^ t, 0] = y[n * 128 : (n + 1) * 128]


def transition_body(
    half, g_ref, x_ref, wo_ref, w1_ref, w2_ref, wl_ref, wr_ref, seq_ref, col_ref, row_ref, *refs
):
    if half:
        _, l0_ref, r0_ref, o_ref, l_ref, r_ref, lacc, racc = refs
        lacc[:, 0:8, :] = l0_ref[...]
        racc[:, 0:8, :] = r0_ref[...]
    else:
        o_ref, lacc, racc = refs
    rows = lax.broadcasted_iota(jnp.int32, (128, 128), 0)
    lanes = lax.broadcasted_iota(jnp.int32, (128, 128), 1)
    own = (rows % 4) == (lanes // 32)
    pick = (
        lax.broadcasted_iota(jnp.int32, (32, 128), 1) // 4
        == lax.broadcasted_iota(jnp.int32, (32, 128), 0)
    ).astype(BF16)
    col, row = col_ref[...].astype(F32), row_ref[...].astype(F32)
    kept = {}

    def project(n):
        gg = jnp.concatenate([g_ref[k, n] for k in range(4)], axis=1)
        y = mm(gg, wo_ref[...])
        mid = jnp.concatenate(
            [x_ref[2 * n + s].astype(F32) + y[:, s * 256 : (s + 1) * 256] for s in range(2)], axis=0
        )
        kept[n] = (mid, lane_norm(mid).astype(BF16))

    def expand(n):
        mid, normed = kept[n]
        kept[n] = (mid, jnp.maximum(mm(normed, w1_ref[...]), 0.0).astype(BF16))

    def shrink(n):
        mid, hidden = kept[n]
        out = (mid + mm(hidden, w2_ref[...])).astype(BF16)
        o_ref[2 * n : 2 * n + 2] = out.reshape(2, 128, 256)
        kept[n] = lane_norm(out).astype(BF16)

    def sides(n):
        z = kept[n]
        left = mm(z, wl_ref[...])
        right = mm_nt(wr_ref[...], z)
        for s in range(2):
            at = slice(s * 128, (s + 1) * 128)
            place = half * 8 + 2 * n + s
            live = seq_ref[place].astype(F32)
            ls = (left[at] * (live * row)).astype(BF16)
            ls = jnp.where(own, ls.astype(F32), 0.0).astype(BF16)
            lacc[:, place, :] = mm(pick, ls)
            racc[:, place, :] = right[:, at] * (live * col)

    stages = (project, expand, shrink, sides)
    for tick in range(4 + len(stages) - 1):
        for k, stage in enumerate(stages):
            if 0 <= tick - k < 4:
                stage(tick - k)
    if half:
        l_ref[...] = lacc[...].astype(BF16)
        r_ref[...] = racc[...].astype(BF16)


def outer_body(
    a0, a1, a2, a2b, a3, b0, b1, b2, b2b, b3, l_ref, c_ref, w_ref, we_ref, inv_ref, live_ref,
    pm_ref, tn_ref, o_ref, left, right, stack, lacc, racc, sem,
):
    r = lax.axis_index("rows")
    copies = []

    def fetch(src, dst):
        copies.append(pltpu.make_async_copy(src, dst, sem.at[len(copies)]))
        copies[-1].start()

    low, high = pl.ds(0, 16), pl.ds(16, 16)
    for k, parts in enumerate(((a0,), (a1,), (a2, a2b), (a3,))):
        n = 4 // len(parts)
        for m, part in enumerate(parts):
            fetch(part, right.at[k, pl.ds(m * n, n), :, low])
    for k, parts in enumerate(((b0,), (b1,), (b2, b2b), (b3,))):
        n = 4 // len(parts)
        for m, part in enumerate(parts):
            fetch(part, right.at[pl.ds(m * n, n), k, :, high])
    for k in range(32):
        src = r ^ k
        for g in range(4):
            left[k * 16 : (k + 1) * 16, g * 128 : (g + 1) * 128] = l_ref[(src % 8) * 4 + src // 8, g]
    lt = left[...].T
    for c in copies:
        c.wait()

    def product(n):
        cols = [right[:, :, :, n * 4 + q].reshape(512, 128) for q in range(4)]
        return mm(lt, jnp.concatenate(cols, axis=1))

    following = product(0)
    for n in range(8):
        o = following
        if n < 7:
            following = product(n + 1)
        o = o.astype(BF16)
        for q in range(4):
            for i in range(16):
                stack[(n * 4 + q) * 32 : (n * 4 + q + 1) * 32, i * 128 : (i + 1) * 128] = o[
                    i * 32 : (i + 1) * 32, q * 128 : (q + 1) * 128
                ]

    kept = {}

    def row4(ref, n):
        return jnp.concatenate([ref[n * 4 + q : n * 4 + q + 1, :] for q in range(4)], axis=1)

    def update(n):
        kept[n] = mm(w_ref[...], stack[:, n * 512 : (n + 1) * 512])

    def merge(n):
        at = slice(n * 512, (n + 1) * 512)
        ct = jnp.concatenate([c_ref[n * 4 + q].astype(F32).T for q in range(4)], axis=1)
        pm = (ct + kept[n] * row4(inv_ref, n)).astype(BF16)
        tn = row_norm(pm.astype(F32)).astype(BF16)
        pm_ref[:, at] = pm
        tn_ref[:, at] = tn
        kept[n] = tn

    def sides(n):
        proj = mm(we_ref[...], kept[n])
        live = row4(live_ref, n)
        ls = sigmoid(proj[128:256]) * proj[0:128] * live
        rs = sigmoid(proj[384:512]) * proj[256:384] * live
        for q in range(4):
            lacc[:, n * 4 + q, :] = ls[:, q * 128 : (q + 1) * 128]
            racc[:, n * 4 + q, :] = rs[:, q * 128 : (q + 1) * 128]

    stages = (update, merge, sides)
    for tick in range(4 + len(stages) - 1):
        for k, stage in enumerate(stages):
            if 0 <= tick - k < 4:
                stage(tick - k)
    o_ref[:, 0] = lacc[...].astype(BF16)
    o_ref[:, 1] = racc[...].astype(BF16)


def triangle_body(x_ref, o_ref, left, right):
    for r in range(32):
        for t in range(4):
            left[r * 16 : (r + 1) * 16, t * 128 : (t + 1) * 128] = x_ref[r * 4 + t, 0]
            right[r * 16 : (r + 1) * 16, t * 128 : (t + 1) * 128] = x_ref[r * 4 + t, 1]
    for q in range(4):
        total = mm_nt(left[q * 128 : (q + 1) * 128, :], right[...])
        for r in range(8):
            for t in range(4):
                o_ref[(q * 8 + r) * 4 + t] = total[
                    r * 16 : (r + 1) * 16, t * 128 : (t + 1) * 128
                ].astype(o_ref.dtype)


def final_body(x_ref, pm_ref, tn_ref, wf_ref, wg_ref, o_ref, normed):
    normed[...] = row_norm(x_ref[...].astype(F32))
    for n in range(4):
        at = slice(n * 512, (n + 1) * 512)
        nt = jnp.concatenate([normed[:, n * 4 + q, :] for q in range(4)], axis=1)
        update = mm(wf_ref[...], nt.astype(BF16))
        gate = sigmoid(mm(wg_ref[...], tn_ref[:, at]))
        res = pm_ref[:, at].astype(F32) + gate * update
        for q in range(4):
            o_ref[n * 4 + q] = res[:, q * 128 : (q + 1) * 128].T.astype(BF16)


def swap_rows(x, unit):
    return lax.ppermute(x, "rows", [(i, i ^ unit) for i in range(32)])


def swap_track(x, unit):
    return lax.ppermute(x, "track", [(i, i ^ unit) for i in range(4)])


def ring_gather(x, unit):
    one, three = swap_rows(x, unit), swap_rows(x, 3 * unit)
    axis = 0 if x.shape[0] > 1 else 1
    half = x.shape[axis] // 2
    first = swap_rows(lax.slice_in_dim(three, 0, half, axis=axis), unit)
    second = swap_rows(lax.slice_in_dim(one, half, 2 * half, axis=axis), 3 * unit)
    return [x, one, first, second, three]


def ring_stack(x, unit):
    own, one, first, second, three = ring_gather(x, unit)
    return jnp.concatenate([own, one, jnp.concatenate([first, second], axis=1), three], axis=0)


def local(
    homolog_embedding,
    couple_embedding,
    amino_validity_flags,
    homolog_validity_flags,
    strand_label,
    focus_four_matrices,
    couple_offset_matrix,
    strand_couple_offset,
    focus_final_matrix,
    transit_expand_matrix,
    transit_shrink_matrix,
    tensor_average_factor_matrices,
    tensor_average_final_matrix,
    trilateral_entry_matrices,
    trilateral_sigmoid_matrix,
    trilateral_final_matrix,
):
    t = lax.axis_index("track")
    r = lax.axis_index("rows")
    x2 = swap_track(homolog_embedding, 2)
    x1 = swap_track(homolog_embedding, 1)
    x3 = swap_track(x2, 1)

    bias_send = call(
        bias_body,
        jax.ShapeDtypeStruct((32, 8, 16, 128), F32),
        [pltpu.VMEM((8, 16, 128), F32), pltpu.SemaphoreType.DMA((32,))],
        in_specs=[SMEM, SMEM] + [VMEM] * 4,
        out_specs=pl.BlockSpec(memory_space=pl.ANY),
        mib=56,
    )(
        strand_label,
        strand_couple_offset,
        couple_embedding,
        couple_offset_matrix.T,
        strand_label.reshape(4, 128),
        amino_validity_flags.reshape(4, 128),
    )
    bias_all = lax.all_to_all(
        bias_send.reshape(128, 2, 16, 128), ("rows", "track"), 0, 0, tiled=True
    )

    w_heads = lax.dynamic_slice_in_dim(
        focus_four_matrices.reshape(256, 4, 8, 32), 2 * t, 2, 2
    ).reshape(256, 256)
    xspec = pl.BlockSpec((2, 128, 256), lambda n: (n, 0, 0))
    xspec4 = pl.BlockSpec((4, 128, 256), lambda n: (n, 0, 0))
    pair_spec = pl.BlockSpec((2, 2, 512, 128), lambda n: (0, n, 0, 0))
    one_spec = pl.BlockSpec((2, 512, 128), lambda n: (n, 0, 0))
    gate_spec = pl.BlockSpec((1, 512, 128), lambda n: (n, 0, 0))
    whole = lambda *shape: pl.BlockSpec(shape, lambda n: (0,) * len(shape))
    query, key, value, gate = call(
        functools.partial(project_body, scale=LOG2E / math.sqrt(32.0)),
        (
            jax.ShapeDtypeStruct((2, 16, 512, 128), BF16),
            jax.ShapeDtypeStruct((16, 512, 128), BF16),
            jax.ShapeDtypeStruct((2, 16, 512, 128), BF16),
            jax.ShapeDtypeStruct((8, 512, 128), BF16),
        ),
        grid=(8,),
        in_specs=[xspec, xspec, xspec, xspec, whole(256, 256)],
        out_specs=(pair_spec, one_spec, pair_spec, gate_spec),
        mib=56,
        cost=pl.CostEstimate(
            flops=16 * 512 * 256 * 256 * 2, bytes_accessed=16 << 20, transcendentals=0
        ),
    )(homolog_embedding, x1, x2, x3, w_heads)
    bias_all = bias_all.reshape(32, 4, 2, 16, 128)
    gated = []
    for half in range(2):
        pair_half = pl.BlockSpec((2, 2, 512, 128), lambda n: (0, n + 4 * half, 0, 0))
        one_half = pl.BlockSpec((2, 512, 128), lambda n: (n + 4 * half, 0, 0))
        gate_half = pl.BlockSpec((1, 512, 128), lambda n: (n + 4 * half, 0, 0))
        mine = call(
            attention_body,
            jax.ShapeDtypeStruct((4, 4, 128, 128), BF16),
            grid=(4,),
            in_specs=[pair_half, one_half, pair_half, gate_half, whole(32, 4, 2, 16, 128)],
            out_specs=pl.BlockSpec((4, 1, 128, 128), lambda n: (0, n, 0, 0)),
            mib=56,
            cost=pl.CostEstimate(
                flops=8 * 2 * 512 * 512 * 64 * 2 * 8, bytes_accessed=8 << 20, transcendentals=4 << 20
            ),
        )(query, key, value, gate, bias_all)
        gated.append(lax.all_to_all(mine, "track", 0, 0, tiled=True))

    res_live = amino_validity_flags.astype(F32)
    seq_live_all = homolog_validity_flags.astype(F32)
    col_live = lax.dynamic_slice_in_dim(res_live, t * 128, 128, 0)
    row_live = lax.dynamic_slice_in_dim(res_live, r * 16, 16, 0)
    seq_live = lax.dynamic_slice_in_dim(seq_live_all, r * 16, 16, 0)
    live_pair = row_live[:, None] * col_live[None, :]
    inv_count = 1.0 / jnp.maximum(jnp.sum(seq_live_all) * live_pair, 1.0)
    eye = jnp.eye(2, dtype=BF16)
    wo = (
        focus_final_matrix.reshape(4, 1, 64, 1, 256) * eye.reshape(1, 2, 1, 2, 1)
    ).reshape(512, 512)
    wl = jnp.tile(tensor_average_factor_matrices[:, :32], (1, 4))
    wr = tensor_average_factor_matrices[:, 32:].T
    weights = (
        wo, transit_expand_matrix, transit_shrink_matrix, wl, wr,
        seq_live, col_live.reshape(1, 128), col_live.reshape(128, 1),
    )
    aligned = jax.ShapeDtypeStruct((16, 128, 256), BF16)
    acc = jax.ShapeDtypeStruct((32, 8, 128), F32)
    side = jax.ShapeDtypeStruct((32, 16, 128), BF16)
    weight_specs = [
        whole(512, 512), whole(256, 1024), whole(1024, 256), whole(256, 128), whole(32, 256),
        SMEM, whole(1, 128), whole(128, 1),
    ]
    g_spec = whole(4, 4, 128, 128)
    cost = pl.CostEstimate(flops=2 << 30, bytes_accessed=4 << 20, transcendentals=0)
    partial, left0, right0 = call(
        functools.partial(transition_body, 0),
        (aligned, acc, acc),
        grid=(1,),
        in_specs=[g_spec, pl.BlockSpec((8, 128, 256), lambda n: (0, 0, 0))] + weight_specs,
        out_specs=(
            pl.BlockSpec((8, 128, 256), lambda n: (0, 0, 0)), whole(32, 8, 128), whole(32, 8, 128)
        ),
        mib=28,
        cost=cost,
    )(gated[0], homolog_embedding, *weights)
    alignment_output, left, right = call(
        functools.partial(transition_body, 1),
        (aligned, side, side),
        [pltpu.VMEM((32, 16, 128), F32), pltpu.VMEM((32, 16, 128), F32)],
        grid=(1,),
        in_specs=[g_spec, pl.BlockSpec((8, 128, 256), lambda n: (1, 0, 0))] + weight_specs
        + [pl.BlockSpec(memory_space=pl.ANY), whole(32, 8, 128), whole(32, 8, 128)],
        out_specs=(
            pl.BlockSpec((8, 128, 256), lambda n: (1, 0, 0)), whole(32, 16, 128), whole(32, 16, 128)
        ),
        input_output_aliases={10: 0},
        mib=28,
        cost=cost,
    )(gated[1], homolog_embedding, *weights, partial, left0, right0)

    swapped = swap_rows(right, 1)
    turn = [
        (k * 32 + z * 8 + m, z * 32 + k * 8 + m) for z in range(4) for m in range(8) for k in range(4)
    ]
    left_turned = lax.ppermute(left, ("track", "rows"), turn)
    swapped, left_turned = lax.optimization_barrier((swapped, left_turned))
    first = ring_gather(ring_stack(jnp.stack([right[:16], swapped[:16]])[None], 2), 8)
    second = ring_gather(ring_stack(jnp.stack([right[16:], swapped[16:]])[None], 8), 2)
    left_send = jnp.broadcast_to(left_turned.reshape(8, 1, 4, 16, 128), (8, 4, 4, 16, 128))
    left_all = lax.all_to_all(
        left_send.reshape(32, 4, 16, 128), ("rows", "track"), 0, 0, tiled=True,
        axis_index_groups=[[z * 32 + n for n in range(32)] for z in range(4)],
    )

    w_out = (
        tensor_average_final_matrix.reshape(32, 32, 128).transpose(2, 1, 0).reshape(128, 1024)
    )
    pair_mid, tri_norm, tri_sides = call(
        outer_body,
        (
            jax.ShapeDtypeStruct((128, 2048), BF16),
            jax.ShapeDtypeStruct((128, 2048), BF16),
            jax.ShapeDtypeStruct((128, 2, 16, 128), BF16),
        ),
        [
            pltpu.VMEM((512, 512), BF16),
            pltpu.VMEM((4, 4, 2, 32, 16, 128), BF16),
            pltpu.VMEM((1024, 2048), BF16),
            pltpu.VMEM((128, 16, 128), F32),
            pltpu.VMEM((128, 16, 128), F32),
            pltpu.SemaphoreType.DMA((10,)),
        ],
        in_specs=[pl.BlockSpec(memory_space=pl.ANY)] * 10 + [VMEM] * 6,
        out_specs=(VMEM,) * 3,
        mib=36,
    )(
        *first, *second, left_all, couple_embedding, w_out,
        trilateral_entry_matrices.T, inv_count, live_pair,
    )

    tri_all = lax.all_to_all(tri_sides, ("rows", "track"), 0, 0, tiled=True)
    tri_sum = call(
        triangle_body,
        jax.ShapeDtypeStruct((128, 16, 128), BF16),
        [pltpu.VMEM((512, 512), BF16), pltpu.VMEM((512, 512), BF16)],
        in_specs=[VMEM],
        out_specs=VMEM,
        mib=16,
    )(tri_all)
    tri_back = lax.all_to_all(tri_sum, ("rows", "track"), 0, 0, tiled=True)
    pair_output = call(
        final_body,
        jax.ShapeDtypeStruct((16, 128, 128), BF16),
        [pltpu.VMEM((128, 16, 128), F32)],
        in_specs=[VMEM] * 5,
        out_specs=VMEM,
        mib=16,
    )(tri_back, pair_mid, tri_norm, trilateral_final_matrix.T, trilateral_sigmoid_matrix.T)
    return (alignment_output, pair_output)


def solution(mesh):
    return jax.shard_map(
        local,
        mesh=mesh,
        in_specs=(P("rows", "track", None), P("rows", "track", None)) + (P(),) * 14,
        out_specs=(P("rows", "track", None), P("rows", "track", None)),
        check_vma=False,
    )
```

```python
import functools
import math

import jax
import jax.numpy as jnp
from jax import lax
from jax.experimental import pallas as pl
from jax.experimental.pallas import tpu as pltpu
from jax.sharding import PartitionSpec as P

norm_eps = 1e-05
mask_fill = 1000000000.0
LOG2E = math.log2(math.e)
F32 = jnp.float32
BF16 = jnp.bfloat16
VMEM = pl.BlockSpec(memory_space=pltpu.VMEM)
SMEM = pl.BlockSpec(memory_space=pltpu.SMEM)


def lane_norm(x):
    x = x.astype(F32)
    x = x - jnp.mean(x, axis=-1, keepdims=True)
    var = jnp.mean(x * x, axis=-1, keepdims=True)
    return x * lax.rsqrt(var + norm_eps)


def row_norm(x):
    x = x - jnp.mean(x, axis=0, keepdims=True)
    var = jnp.mean(x * x, axis=0, keepdims=True)
    return x * lax.rsqrt(var + norm_eps)


def mm(a, b):
    return jnp.dot(a, b, preferred_element_type=F32)


def mm_nt(a, b):
    return lax.dot_general(a, b, (((1,), (1,)), ((), ())), preferred_element_type=F32)


def sigmoid(x):
    return 1.0 / (1.0 + jnp.exp(-x))


def call(body, outs, scratch=(), **kw):
    cost = kw.pop("cost", None)
    mib = kw.pop("mib")
    return pl.pallas_call(
        body,
        out_shape=outs,
        scratch_shapes=list(scratch),
        cost_estimate=cost,
        compiler_params=pltpu.CompilerParams(vmem_limit_bytes=mib * 1024 * 1024),
        **kw,
    )


def bias_body(chain_ref, so_ref, c_ref, w_ref, cols_ref, res_ref, o_ref, out, sem):
    t, r = lax.axis_index("track"), lax.axis_index("rows")
    rows = c_ref.shape[0]
    w = w_ref[...] * LOG2E
    hi = w.astype(BF16).astype(F32)
    mid = (w - hi).astype(BF16).astype(F32)
    w = jnp.concatenate([hi, mid, w - hi - mid], axis=0).astype(BF16)
    pn = lane_norm(c_ref[...]).astype(BF16).reshape(rows * 128, 128)
    b = mm_nt(w, pn)
    b = b[0:8] + b[8:16] + b[16:24]
    head = lax.broadcasted_iota(jnp.int32, (8, 1), 0)
    so = jnp.zeros((8, 1), F32)
    for h in range(8):
        so = jnp.where(head == h, so_ref[h], so)
    so = so * LOG2E
    chain = cols_ref[pl.ds(t, 1), :]
    mask = (res_ref[pl.ds(t, 1), :].astype(F32) - 1.0) * (mask_fill * LOG2E)
    for i in range(rows):
        same = (chain == chain_ref[r * rows + i]).astype(F32)
        out[:, i, :] = b[:, i * 128 : (i + 1) * 128] + so * same + mask
    copies = [pltpu.make_async_copy(out, o_ref.at[n], sem.at[n]) for n in range(32)]
    for c in copies:
        c.start()
    for c in copies:
        c.wait()


def project_body(x0, x1, x2, x3, w_ref, q_ref, k_ref, v_ref, g_ref, *, scale):
    lane = lax.broadcasted_iota(jnp.int32, (1, 128), 1)
    factor = jnp.where(lane < 64, scale, 1.0)
    gates = []
    for s in range(2):
        xn = jnp.concatenate([lane_norm(x[s]).astype(BF16) for x in (x0, x1, x2, x3)], axis=0)
        qkvg = mm(xn, w_ref[...])
        qk = qkvg[:, :128] * factor
        vg = qkvg[:, 128:].astype(BF16).astype(F32)
        k_ref[s] = qk.astype(BF16)
        moved = pltpu.roll(qk, 64, 1)
        for h in range(2):
            klanes = (lane >= 64 + 32 * h) & (lane < 96 + 32 * h)
            q_ref[h, s] = jnp.where(klanes, moved, 0.0).astype(BF16)
            vlanes = (lane >= 32 * h) & (lane < 32 + 32 * h)
            v_ref[h, s] = jnp.where(vlanes, vg, 1.0).astype(BF16)
        gates.append(vg)
    g_ref[0] = jnp.where(lane < 64, pltpu.roll(gates[0], 64, 1), gates[1]).astype(BF16)


def attention_body(q_ref, k_ref, v_ref, g_ref, b_ref, o_ref):
    t = lax.axis_index("track")
    size = 256
    blocks = [(s, k, h) for s in range(2) for k in range(512 // size) for h in range(2)]

    def bias(k, h):
        tall = []
        for ki in range(k * size // 128, (k + 1) * size // 128):
            rows = pl.ds(pl.multiple_of((ki ^ t) * 8, 8), 8)
            wide = [b_ref[rows, kj ^ t, h].reshape(128, 128) for kj in range(4)]
            tall.append(jnp.concatenate(wide, axis=1))
        return jnp.concatenate(tall, axis=0)

    def score(block):
        s, k, h = block
        return mm_nt(q_ref[h, s, k * size : (k + 1) * size], k_ref[s]) + bias(k, h)

    outs = {}

    def weigh(block, p):
        s, k, h = block
        outs[block] = mm(p, v_ref[h, s])

    following, held = score(blocks[0]), None
    for n, block in enumerate(blocks):
        now = following
        if n + 1 < len(blocks):
            following = score(blocks[n + 1])
        p = jnp.exp2(now - jnp.max(now, axis=-1, keepdims=True)).astype(BF16)
        if held is not None:
            weigh(*held)
        held = (block, p)
    weigh(*held)
    head0 = lax.broadcasted_iota(jnp.int32, (1, 128), 1) < 32
    for k in range(512 // size):
        at = slice(k * size, (k + 1) * size)
        parts = []
        for s in range(2):
            o0, o1 = outs[(s, k, 0)], outs[(s, k, 1)]
            num = jnp.where(head0, o0, o1)[:, :64]
            den = jnp.where(head0[:, :64], o0[:, 64:], o1[:, 64:])
            parts.append(num / den)
        y = jnp.concatenate(parts, axis=1) * sigmoid(g_ref[0, at].astype(F32))
        y = y.astype(BF16)
        for n in range(size // 128):
            o_ref[(k * (size // 128) + n) ^ t, 0] = y[n * 128 : (n + 1) * 128]


def transition_body(
    half, g_ref, x_ref, wo_ref, w1_ref, w2_ref, wl_ref, wr_ref, seq_ref, col_ref, row_ref, *refs
):
    if half:
        _, l0_ref, r0_ref, o_ref, l_ref, r_ref, lacc, racc = refs
        lacc[:, 0:8, :] = l0_ref[...]
        racc[:, 0:8, :] = r0_ref[...]
    else:
        o_ref, lacc, racc = refs
    rows = lax.broadcasted_iota(jnp.int32, (128, 128), 0)
    lanes = lax.broadcasted_iota(jnp.int32, (128, 128), 1)
    own = (rows % 4) == (lanes // 32)
    pick = (
        lax.broadcasted_iota(jnp.int32, (32, 128), 1) // 4
        == lax.broadcasted_iota(jnp.int32, (32, 128), 0)
    ).astype(BF16)
    col, row = col_ref[...].astype(F32), row_ref[...].astype(F32)
    kept = {}

    def project(n):
        gg = jnp.concatenate([g_ref[k, n] for k in range(4)], axis=1)
        y = mm(gg, wo_ref[...])
        mid = jnp.concatenate(
            [x_ref[2 * n + s].astype(F32) + y[:, s * 256 : (s + 1) * 256] for s in range(2)], axis=0
        )
        kept[n] = (mid, lane_norm(mid).astype(BF16))

    def expand(n):
        mid, normed = kept[n]
        kept[n] = (mid, jnp.maximum(mm(normed, w1_ref[...]), 0.0).astype(BF16))

    def shrink(n):
        mid, hidden = kept[n]
        out = (mid + mm(hidden, w2_ref[...])).astype(BF16)
        o_ref[2 * n : 2 * n + 2] = out.reshape(2, 128, 256)
        kept[n] = lane_norm(out).astype(BF16)

    def sides(n):
        z = kept[n]
        left = mm(z, wl_ref[...])
        right = mm_nt(wr_ref[...], z)
        for s in range(2):
            at = slice(s * 128, (s + 1) * 128)
            place = half * 8 + 2 * n + s
            live = seq_ref[place].astype(F32)
            ls = (left[at] * (live * row)).astype(BF16)
            ls = jnp.where(own, ls.astype(F32), 0.0).astype(BF16)
            lacc[:, place, :] = mm(pick, ls)
            racc[:, place, :] = right[:, at] * (live * col)

    stages = (project, expand, shrink, sides)
    for tick in range(4 + len(stages) - 1):
        for k, stage in enumerate(stages):
            if 0 <= tick - k < 4:
                stage(tick - k)
    if half:
        l_ref[...] = lacc[...].astype(BF16)
        r_ref[...] = racc[...].astype(BF16)


def outer_body(
    a0, a1, a2, a3, b0, b1, b2, b3, l_ref, c_ref, w_ref, we_ref, inv_ref, live_ref,
    pm_ref, tn_ref, o_ref, left, right, stack, lacc, racc, sem,
):
    r = lax.axis_index("rows")
    copies = []

    def fetch(src, dst):
        copies.append(pltpu.make_async_copy(src, dst, sem.at[len(copies)]))
        copies[-1].start()

    low, high = pl.ds(0, 16), pl.ds(16, 16)
    for k, part in enumerate((a0, a1, a2, a3)):
        fetch(part, right.at[k, :, :, low])
    for k, part in enumerate((b0, b1, b2, b3)):
        fetch(part, right.at[:, k, :, high])
    for k in range(32):
        src = r ^ k
        for g in range(4):
            left[k * 16 : (k + 1) * 16, g * 128 : (g + 1) * 128] = l_ref[(src % 8) * 4 + src // 8, g]
    lt = left[...].T

    def product(n):
        if n in (0, 4):
            for c in copies[n : n + 4]:
                c.wait()
        cols = [right[:, :, :, n * 4 + q].reshape(512, 128) for q in range(4)]
        return mm(lt, jnp.concatenate(cols, axis=1))

    following = product(0)
    for n in range(8):
        o = following
        if n < 7:
            following = product(n + 1)
        o = o.astype(BF16)
        for q in range(4):
            for i in range(16):
                stack[(n * 4 + q) * 32 : (n * 4 + q + 1) * 32, i * 128 : (i + 1) * 128] = o[
                    i * 32 : (i + 1) * 32, q * 128 : (q + 1) * 128
                ]

    kept = {}

    def row4(ref, n):
        return jnp.concatenate([ref[n * 4 + q : n * 4 + q + 1, :] for q in range(4)], axis=1)

    def update(n):
        kept[n] = mm(w_ref[...], stack[:, n * 512 : (n + 1) * 512])

    def merge(n):
        at = slice(n * 512, (n + 1) * 512)
        ct = jnp.concatenate([c_ref[n * 4 + q].astype(F32).T for q in range(4)], axis=1)
        pm = (ct + kept[n] * row4(inv_ref, n)).astype(BF16)
        tn = row_norm(pm.astype(F32)).astype(BF16)
        pm_ref[:, at] = pm
        tn_ref[:, at] = tn
        kept[n] = tn

    def sides(n):
        proj = mm(we_ref[...], kept[n])
        live = row4(live_ref, n)
        ls = sigmoid(proj[128:256]) * proj[0:128] * live
        rs = sigmoid(proj[384:512]) * proj[256:384] * live
        for q in range(4):
            lacc[:, n * 4 + q, :] = ls[:, q * 128 : (q + 1) * 128]
            racc[:, n * 4 + q, :] = rs[:, q * 128 : (q + 1) * 128]

    stages = (update, merge, sides)
    for tick in range(4 + len(stages) - 1):
        for k, stage in enumerate(stages):
            if 0 <= tick - k < 4:
                stage(tick - k)
    o_ref[:, 0] = lacc[...].astype(BF16)
    o_ref[:, 1] = racc[...].astype(BF16)


def triangle_body(x_ref, o_ref, left, right):
    for r in range(32):
        for t in range(4):
            left[r * 16 : (r + 1) * 16, t * 128 : (t + 1) * 128] = x_ref[r * 4 + t, 0]
            right[r * 16 : (r + 1) * 16, t * 128 : (t + 1) * 128] = x_ref[r * 4 + t, 1]
    for q in range(4):
        total = mm_nt(left[q * 128 : (q + 1) * 128, :], right[...])
        for r in range(8):
            for t in range(4):
                o_ref[(q * 8 + r) * 4 + t] = total[
                    r * 16 : (r + 1) * 16, t * 128 : (t + 1) * 128
                ].astype(o_ref.dtype)


def final_body(x_ref, pm_ref, tn_ref, wf_ref, wg_ref, o_ref, normed):
    normed[...] = row_norm(x_ref[...].astype(F32))
    for n in range(4):
        at = slice(n * 512, (n + 1) * 512)
        nt = jnp.concatenate([normed[:, n * 4 + q, :] for q in range(4)], axis=1)
        update = mm(wf_ref[...], nt.astype(BF16))
        gate = sigmoid(mm(wg_ref[...], tn_ref[:, at]))
        res = pm_ref[:, at].astype(F32) + gate * update
        for q in range(4):
            o_ref[n * 4 + q] = res[:, q * 128 : (q + 1) * 128].T.astype(BF16)


def swap_rows(x, unit):
    return lax.ppermute(x, "rows", [(i, i ^ unit) for i in range(32)])


def swap_track(x, unit):
    return lax.ppermute(x, "track", [(i, i ^ unit) for i in range(4)])


def ring_gather(x, unit):
    three, one = swap_rows(x, 3 * unit), swap_rows(x, unit)
    return [x, one, swap_rows(three, unit), three]


def local(
    homolog_embedding,
    couple_embedding,
    amino_validity_flags,
    homolog_validity_flags,
    strand_label,
    focus_four_matrices,
    couple_offset_matrix,
    strand_couple_offset,
    focus_final_matrix,
    transit_expand_matrix,
    transit_shrink_matrix,
    tensor_average_factor_matrices,
    tensor_average_final_matrix,
    trilateral_entry_matrices,
    trilateral_sigmoid_matrix,
    trilateral_final_matrix,
):
    t = lax.axis_index("track")
    r = lax.axis_index("rows")
    x2 = swap_track(homolog_embedding, 2)
    x1 = swap_track(homolog_embedding, 1)
    x3 = swap_track(x2, 1)

    bias_send = call(
        bias_body,
        jax.ShapeDtypeStruct((32, 8, 16, 128), F32),
        [pltpu.VMEM((8, 16, 128), F32), pltpu.SemaphoreType.DMA((32,))],
        in_specs=[SMEM, SMEM] + [VMEM] * 4,
        out_specs=pl.BlockSpec(memory_space=pl.ANY),
        mib=56,
    )(
        strand_label,
        strand_couple_offset,
        couple_embedding,
        couple_offset_matrix.T,
        strand_label.reshape(4, 128),
        amino_validity_flags.reshape(4, 128),
    )
    bias_all = lax.all_to_all(
        bias_send.reshape(128, 2, 16, 128), ("rows", "track"), 0, 0, tiled=True
    )

    w_heads = lax.dynamic_slice_in_dim(
        focus_four_matrices.reshape(256, 4, 8, 32), 2 * t, 2, 2
    ).reshape(256, 256)
    xspec = pl.BlockSpec((2, 128, 256), lambda n: (n, 0, 0))
    xspec4 = pl.BlockSpec((4, 128, 256), lambda n: (n, 0, 0))
    pair_spec = pl.BlockSpec((2, 2, 512, 128), lambda n: (0, n, 0, 0))
    one_spec = pl.BlockSpec((2, 512, 128), lambda n: (n, 0, 0))
    gate_spec = pl.BlockSpec((1, 512, 128), lambda n: (n, 0, 0))
    whole = lambda *shape: pl.BlockSpec(shape, lambda n: (0,) * len(shape))
    query, key, value, gate = call(
        functools.partial(project_body, scale=LOG2E / math.sqrt(32.0)),
        (
            jax.ShapeDtypeStruct((2, 16, 512, 128), BF16),
            jax.ShapeDtypeStruct((16, 512, 128), BF16),
            jax.ShapeDtypeStruct((2, 16, 512, 128), BF16),
            jax.ShapeDtypeStruct((8, 512, 128), BF16),
        ),
        grid=(8,),
        in_specs=[xspec, xspec, xspec, xspec, whole(256, 256)],
        out_specs=(pair_spec, one_spec, pair_spec, gate_spec),
        mib=56,
        cost=pl.CostEstimate(
            flops=16 * 512 * 256 * 256 * 2, bytes_accessed=16 << 20, transcendentals=0
        ),
    )(homolog_embedding, x1, x2, x3, w_heads)
    bias_all = bias_all.reshape(32, 4, 2, 16, 128)
    gated = []
    for half in range(2):
        pair_half = pl.BlockSpec((2, 2, 512, 128), lambda n: (0, n + 4 * half, 0, 0))
        one_half = pl.BlockSpec((2, 512, 128), lambda n: (n + 4 * half, 0, 0))
        gate_half = pl.BlockSpec((1, 512, 128), lambda n: (n + 4 * half, 0, 0))
        mine = call(
            attention_body,
            jax.ShapeDtypeStruct((4, 4, 128, 128), BF16),
            grid=(4,),
            in_specs=[pair_half, one_half, pair_half, gate_half, whole(32, 4, 2, 16, 128)],
            out_specs=pl.BlockSpec((4, 1, 128, 128), lambda n: (0, n, 0, 0)),
            mib=56,
            cost=pl.CostEstimate(
                flops=8 * 2 * 512 * 512 * 64 * 2 * 8, bytes_accessed=8 << 20, transcendentals=4 << 20
            ),
        )(query, key, value, gate, bias_all)
        gated.append(lax.all_to_all(mine, "track", 0, 0, tiled=True))

    res_live = amino_validity_flags.astype(F32)
    seq_live_all = homolog_validity_flags.astype(F32)
    col_live = lax.dynamic_slice_in_dim(res_live, t * 128, 128, 0)
    row_live = lax.dynamic_slice_in_dim(res_live, r * 16, 16, 0)
    seq_live = lax.dynamic_slice_in_dim(seq_live_all, r * 16, 16, 0)
    live_pair = row_live[:, None] * col_live[None, :]
    inv_count = 1.0 / jnp.maximum(jnp.sum(seq_live_all) * live_pair, 1.0)
    eye = jnp.eye(2, dtype=BF16)
    wo = (
        focus_final_matrix.reshape(4, 1, 64, 1, 256) * eye.reshape(1, 2, 1, 2, 1)
    ).reshape(512, 512)
    wl = jnp.tile(tensor_average_factor_matrices[:, :32], (1, 4))
    wr = tensor_average_factor_matrices[:, 32:].T
    weights = (
        wo, transit_expand_matrix, transit_shrink_matrix, wl, wr,
        seq_live, col_live.reshape(1, 128), col_live.reshape(128, 1),
    )
    aligned = jax.ShapeDtypeStruct((16, 128, 256), BF16)
    acc = jax.ShapeDtypeStruct((32, 8, 128), F32)
    side = jax.ShapeDtypeStruct((32, 16, 128), BF16)
    weight_specs = [
        whole(512, 512), whole(256, 1024), whole(1024, 256), whole(256, 128), whole(32, 256),
        SMEM, whole(1, 128), whole(128, 1),
    ]
    g_spec = whole(4, 4, 128, 128)
    cost = pl.CostEstimate(flops=2 << 30, bytes_accessed=4 << 20, transcendentals=0)
    partial, left0, right0 = call(
        functools.partial(transition_body, 0),
        (aligned, acc, acc),
        grid=(1,),
        in_specs=[g_spec, pl.BlockSpec((8, 128, 256), lambda n: (0, 0, 0))] + weight_specs,
        out_specs=(
            pl.BlockSpec((8, 128, 256), lambda n: (0, 0, 0)), whole(32, 8, 128), whole(32, 8, 128)
        ),
        mib=28,
        cost=cost,
    )(gated[0], homolog_embedding, *weights)
    alignment_output, left, right = call(
        functools.partial(transition_body, 1),
        (aligned, side, side),
        [pltpu.VMEM((32, 16, 128), F32), pltpu.VMEM((32, 16, 128), F32)],
        grid=(1,),
        in_specs=[g_spec, pl.BlockSpec((8, 128, 256), lambda n: (1, 0, 0))] + weight_specs
        + [pl.BlockSpec(memory_space=pl.ANY), whole(32, 8, 128), whole(32, 8, 128)],
        out_specs=(
            pl.BlockSpec((8, 128, 256), lambda n: (1, 0, 0)), whole(32, 16, 128), whole(32, 16, 128)
        ),
        input_output_aliases={10: 0},
        mib=28,
        cost=cost,
    )(gated[1], homolog_embedding, *weights, partial, left0, right0)

    swapped = swap_rows(right, 1)
    turn = [
        (k * 32 + z * 8 + m, z * 32 + k * 8 + m) for z in range(4) for m in range(8) for k in range(4)
    ]
    left_turned = lax.ppermute(left, ("track", "rows"), turn)
    swapped, left_turned = lax.optimization_barrier((swapped, left_turned))
    first = jnp.stack(ring_gather(jnp.stack([right[:16], swapped[:16]]), 2))
    second = jnp.stack(ring_gather(jnp.stack([right[16:], swapped[16:]]), 8))
    first = ring_gather(first, 8)
    second = ring_gather(second, 2)
    left_send = jnp.broadcast_to(left_turned.reshape(8, 1, 4, 16, 128), (8, 4, 4, 16, 128))
    left_all = lax.all_to_all(
        left_send.reshape(32, 4, 16, 128), ("rows", "track"), 0, 0, tiled=True,
        axis_index_groups=[[z * 32 + n for n in range(32)] for z in range(4)],
    )

    w_out = (
        tensor_average_final_matrix.reshape(32, 32, 128).transpose(2, 1, 0).reshape(128, 1024)
    )
    pair_mid, tri_norm, tri_sides = call(
        outer_body,
        (
            jax.ShapeDtypeStruct((128, 2048), BF16),
            jax.ShapeDtypeStruct((128, 2048), BF16),
            jax.ShapeDtypeStruct((128, 2, 16, 128), BF16),
        ),
        [
            pltpu.VMEM((512, 512), BF16),
            pltpu.VMEM((4, 4, 2, 32, 16, 128), BF16),
            pltpu.VMEM((1024, 2048), BF16),
            pltpu.VMEM((128, 16, 128), F32),
            pltpu.VMEM((128, 16, 128), F32),
            pltpu.SemaphoreType.DMA((8,)),
        ],
        in_specs=[pl.BlockSpec(memory_space=pl.ANY)] * 8 + [VMEM] * 6,
        out_specs=(VMEM,) * 3,
        mib=36,
    )(
        *first, *second, left_all, couple_embedding, w_out,
        trilateral_entry_matrices.T, inv_count, live_pair,
    )

    tri_all = lax.all_to_all(tri_sides, ("rows", "track"), 0, 0, tiled=True)
    tri_sum = call(
        triangle_body,
        jax.ShapeDtypeStruct((128, 16, 128), BF16),
        [pltpu.VMEM((512, 512), BF16), pltpu.VMEM((512, 512), BF16)],
        in_specs=[VMEM],
        out_specs=VMEM,
        mib=16,
    )(tri_all)
    tri_back = lax.all_to_all(tri_sum, ("rows", "track"), 0, 0, tiled=True)
    pair_output = call(
        final_body,
        jax.ShapeDtypeStruct((16, 128, 128), BF16),
        [pltpu.VMEM((128, 16, 128), F32)],
        in_specs=[VMEM] * 5,
        out_specs=VMEM,
        mib=56,
    )(tri_back, pair_mid, tri_norm, trilateral_final_matrix.T, trilateral_sigmoid_matrix.T)
    return (alignment_output, pair_output)


def solution(mesh):
    return jax.shard_map(
        local,
        mesh=mesh,
        in_specs=(P("rows", "track", None), P("rows", "track", None)) + (P(),) * 14,
        out_specs=(P("rows", "track", None), P("rows", "track", None)),
        check_vma=False,
    )
```
